256 devices in a mesh: ctx: 32 (over y, z_hi, x), tp: 8 (over z_lo, core).
Axes of the slice: x: 4, y: 4, z: 8 (z_hi: 2, z_lo: 4; z = z_hi * 4 + z_lo), core: 2. Of those that a mesh axis runs over, the one named last changes fastest.
Arguments:
- queries: bfloat16 [2048, 16384], P('tp', 'ctx'), may hold values from -6 to 6
- key_branch: bfloat16 [2048, 16384], P('tp', 'ctx'), may hold values from -6 to 6
- value_branch: bfloat16 [2048, 16384], P('tp', 'ctx'), may hold values from -6 to 6
- filters: bfloat16 [256, 16384], P(None, 'ctx'), may hold values from -6 to 6
- cotangent: bfloat16 [2048, 16384], P('tp', 'ctx'), may hold values from -6 to 6
Outputs:
- grad_queries: bfloat16 [2048, 16384], P('tp', 'ctx')
- grad_keys: bfloat16 [2048, 16384], P('tp', 'ctx')
- grad_values: bfloat16 [2048, 16384], P('tp', 'ctx')
- grad_filters: bfloat16 [256, 16384], P(None, 'ctx')
The draws below stay inside these ranges and needn't reach their ends.
All inputs are finite; a program needn't handle non-finite values.
Results may differ from the reference program's by a relative error of at most 0.024.
Values may be sent and summed in bfloat16 or wider, within the bound.
A program may use at most 64 MiB of HBM per device.

```python
import jax
import jax.numpy as jnp
from jax import lax

FILTERS = 256
SEQ = 16384
CHANNELS = 2048
N_TP = 8


def block_levels(key, dims, pieces, least, high):
    loudness, own = 1.0, jax.random.fold_in(key, 6)
    for dim, shards_of in pieces:
        steps = jnp.exp(jax.random.uniform(jax.random.fold_in(own, dim), (shards_of,), jnp.float32, least / len(pieces), high / len(pieces)))
        loudness = loudness * jnp.repeat(steps, dims[dim] // shards_of).reshape([-1 if axis == dim else 1 for axis in range(len(dims))])
    return loudness


def centred(rng, shape, width, bound, split=(), dtype=jnp.bfloat16):
    gain = block_levels(rng, shape, split, -0.22, 0.18) if split else 1.0
    entries = jax.random.normal(rng, shape, jnp.float32) * width * gain
    return jnp.minimum(jnp.maximum(entries, -bound), bound).astype(dtype)


def setup_inputs(seed: int = 0) -> dict:
    splits = jax.random.split(jax.random.key(seed), 6)
    queries = centred(splits[0], (CHANNELS, SEQ), 1.0, 6.0, ((0, 8), (1, 32)))
    key_branch = centred(splits[1], (CHANNELS, SEQ), 1.0, 6.0, ((0, 8), (1, 32)))
    value_branch = centred(splits[2], (CHANNELS, SEQ), 1.0, 6.0, ((0, 8), (1, 32)))
    filters = centred(splits[3], (FILTERS, SEQ), 1.0, 6.0, ((1, 32),))
    cotangent = centred(splits[4], (CHANNELS, SEQ), 1.0, 6.0, ((0, 8), (1, 32)))
    return dict(queries=queries, key_branch=key_branch, value_branch=value_branch, filters=filters, cotangent=cotangent)


def reference(queries, key_branch, value_branch, filters, cotangent):
    gated = (key_branch.astype(jnp.float32) * value_branch.astype(jnp.float32)).astype(jnp.bfloat16)
    grad_conv = (cotangent.astype(jnp.float32) * queries.astype(jnp.float32)).astype(jnp.bfloat16)
    tap_scale = SEQ ** -0.5
    taps = filters.astype(jnp.float32) * tap_scale
    fft_length = 2 * SEQ
    tap_spec = jnp.fft.rfft(taps, n=fft_length, axis=1)

    def per_group(pair):
        gated_block, grad_block = pair
        gated_spec = jnp.fft.rfft(gated_block.astype(jnp.float32), n=fft_length, axis=1)
        grad_spec = jnp.fft.rfft(grad_block.astype(jnp.float32), n=fft_length, axis=1)
        conv_out = jnp.fft.irfft(gated_spec * tap_spec, n=fft_length, axis=1)[:, :SEQ]
        grad_gated = jnp.fft.irfft(jnp.conj(tap_spec) * grad_spec, n=fft_length, axis=1)[:, :SEQ]
        tap_terms = jnp.fft.irfft(jnp.conj(gated_spec) * grad_spec, n=fft_length, axis=1)[:, :SEQ]
        return conv_out.astype(jnp.float32), grad_gated.astype(jnp.float32), tap_terms.astype(jnp.float32)

    conv_out, grad_gated, tap_terms = lax.map(
        per_group, (gated.reshape(N_TP, FILTERS, SEQ), grad_conv.reshape(N_TP, FILTERS, SEQ)))
    conv_low = conv_out.reshape(CHANNELS, SEQ).astype(jnp.bfloat16)
    grad_low = grad_gated.reshape(CHANNELS, SEQ).astype(jnp.bfloat16)
    grad_queries = (cotangent.astype(jnp.float32) * conv_low.astype(jnp.float32)).astype(jnp.bfloat16)
    grad_keys = (grad_low.astype(jnp.float32) * value_branch.astype(jnp.float32)).astype(jnp.bfloat16)
    grad_values = (grad_low.astype(jnp.float32) * key_branch.astype(jnp.float32)).astype(jnp.bfloat16)
    grad_filters = (jnp.sum(tap_terms, axis=0) * tap_scale).astype(jnp.bfloat16)
    return grad_queries, grad_keys, grad_values, grad_filters
```

```python
import functools

import jax
import jax.numpy as jnp
import ml_dtypes
import numpy as np
from jax import lax
from jax.experimental import pallas as pl
from jax.experimental.pallas import tpu as pltpu
from jax.sharding import PartitionSpec as P

MESH = pl.DeviceIdType.MESH
F32 = jnp.float32
BF16 = jnp.bfloat16

SEQ = 16384
CTX = 32
TP = 8
TOK = SEQ // CTX
R = 128
Q = TOK // R
SCALE = 2.0**-21


def tables():
    k = np.arange(R, dtype=np.float64)[:, None]
    n = np.arange(R, dtype=np.float64)[None, :]
    angle = 2 * np.pi * (k + 0.25) * n / R
    outer = np.concatenate([np.cos(angle), -np.sin(angle)], 0)
    order = np.arange(R).reshape(CTX, Q).T.reshape(-1)
    twist = 2 * np.pi * (k + 0.25) * n / SEQ
    inner = 2 * np.pi * ((k * n) % R) / R
    c, s = np.cos(inner), np.sin(inner)
    fwd = np.block([[c, -s], [s, c]])
    as_bf16 = lambda t: np.asarray(t, np.float32).astype(ml_dtypes.bfloat16)
    return (
        as_bf16(outer[:, order]),
        np.stack([np.cos(twist), np.sin(twist)]).astype(np.float32),
        as_bf16(fwd),
        as_bf16(fwd.T),
        as_bf16(outer.T[order]),
        as_bf16(outer.T),
    )


def dot(a, b):
    return jnp.dot(a, b, preferred_element_type=F32)


def exchange_kernel(
    q_ref, k_ref, v_ref, f_ref, c_ref, e1, tw, fw, fi, e1q, e1n,
    out_ref, fil_ref,
    snd, rcv, osnd, orcv, fs, fsnd, fall, sbuf, sf, spec, hspec, ytap, tarcv, tbsnd, tbrcv, tbown,
    csnd, crcv, cflat, dbuf,
    s_in, r_in, s_f, r_f, s_out, r_out, s_c, r_c, s_z, r_z, s_d, r_d, s_x, r_x,
):
    me = lax.axis_index("ctx")
    tp = lax.axis_index("tp")
    core = tp % 2
    zlo = tp // 2
    mx, mz, my = me % 4, (me // 4) % 2, me // 8
    mate = zlo * 2 + 1 - core

    def peer(i):
        dz = 1 - i // 16
        return ((my + (i // 4) % 4) % 4) * 8 + ((mz + dz) % 2) * 4 + (mx + i % 4) % 4

    def others(body):
        lax.fori_loop(0, 16, lambda i, _: (body(i), 0)[1], 0)
        lax.fori_loop(17, 32, lambda i, _: (body(i), 0)[1], 0)

    def chip(dz):
        return ((zlo + dz) % 4) * 2 + core

    def remote(src, dst, ss, rs, c, t):
        return pltpu.make_async_remote_copy(
            src_ref=src, dst_ref=dst, send_sem=ss, recv_sem=rs, device_id=(c, t), device_id_type=MESH)

    barrier = pltpu.get_barrier_semaphore()

    def greet(c, t):
        pl.semaphore_signal(barrier, inc=1, device_id=(c, t), device_id_type=MESH)

    others(lambda i: greet(peer(i), tp))
    greet(me, mate)
    for dz in (1, 2, 3):
        greet(me, chip(dz))

    def gates(j, _):
        rows = pl.ds(pl.multiple_of(j * 16, 16), 16)
        g = k_ref[rows, :].astype(F32) * v_ref[rows, :].astype(F32)
        d = c_ref[rows, :].astype(F32) * q_ref[rows, :].astype(F32)
        snd[2 * j] = jnp.concatenate([g[:8], d[:8]], 0).astype(BF16)
        snd[2 * j + 1] = jnp.concatenate([g[8:], d[8:]], 0).astype(BF16)
        return 0

    lax.fori_loop(0, CTX // 2, gates, 0)
    rcv[me] = snd[me]
    pl.semaphore_wait(barrier, 35)

    def in_copy(i):
        c = peer(i)
        return remote(snd.at[c], rcv.at[me], s_in.at[i], r_in.at[i], c, tp)

    others(lambda i: in_copy(i).start())

    for q in range(Q):
        fs[q] = f_ref[:, q * R:(q + 1) * R].astype(F32)
    for q in range(Q):
        for f in range(4):
            sf[0, pl.ds(q * 4 + f, CTX, stride=16), :] = fs[q, pl.ds(core * 4 + f, CTX, stride=8), :]
    for c in range(CTX):
        fsnd[c] = sf[0, c * 16:(c + 1) * 16, :].astype(BF16)
    fall[core, me] = fsnd[me]

    def f_copy(i):
        c = peer(i)
        return remote(fsnd.at[c], fall.at[core, me], s_f.at[i], r_f.at[i], c, tp)

    others(lambda i: f_copy(i).start())

    def forward(x):
        y = dot(e1[...], x)
        yr, yi = y[:R], y[R:]
        tc, ts = tw[0], tw[1]
        left = jnp.concatenate([(yr * tc + yi * ts).astype(BF16), (yi * tc - yr * ts).astype(BF16)], 1)
        return dot(left, fw[...])

    def inverse(pr, pi, out):
        u = dot(jnp.concatenate([pr.astype(BF16), pi.astype(BF16)], 1), fi[...])
        ur, ui = u[:, :R], u[:, R:]
        tc, ts = tw[0], tw[1]
        v = jnp.concatenate([(ur * tc - ui * ts).astype(BF16), (ui * tc + ur * ts).astype(BF16)], 0)
        return dot(out[...], v)

    others(lambda i: in_copy(i).wait_recv())

    def widen(c, _):
        v = rcv[c].astype(F32)
        for q in range(Q):
            sbuf[q, pl.ds(pl.multiple_of(c * 16, 16), 16), :] = v[:, q * R:(q + 1) * R]
        return 0

    lax.fori_loop(0, CTX, widen, 0)
    for r in range(16):
        x = jnp.concatenate([sbuf[q, pl.ds(r, CTX, stride=16), :] for q in range(Q)], 0)
        spec[r] = forward(x.astype(BF16))

    others(lambda i: f_copy(i).wait_recv())
    mate_f = remote(fall.at[core], fall.at[core], s_x.at[0], r_x.at[0], me, mate)
    mate_f.start()

    def tap(ch, _):
        g, d = spec[ch], spec[ch + 8]
        gr, gi, dr, di = g[:, :R], g[:, R:], d[:, :R], d[:, R:]
        ytap[ch] = inverse(gr * dr + gi * di, gr * di - gi * dr, e1n)
        return 0

    lax.fori_loop(0, 8, tap, 0)
    mate_t = remote(ytap.at[pl.ds((1 - core) * 4, 4)], tarcv, s_x.at[1], r_x.at[1], me, mate)
    mate_t.start()

    mate_f.wait_recv()
    for j in range(2):
        for c in range(CTX):
            sf[j, c * 16:(c + 1) * 16, :] = fall[j, c].astype(F32)
    for j in range(2):
        for f in range(4):
            x = jnp.concatenate([sf[j, pl.ds(q * 4 + f, CTX, stride=16), :] for q in range(Q)], 0)
            hspec[j * 4 + f] = forward(x.astype(BF16))

    mate_t.wait_recv()
    for f in range(4):
        tbsnd[f] = (ytap[core * 4 + f] + tarcv[f]).astype(BF16)

    def z_copy(dz):
        to = (zlo + dz) % 4
        return remote(tbsnd.at[to], tbrcv.at[dz], s_z.at[dz], r_z.at[dz], me, chip(dz))

    for dz in (1, 2, 3):
        z_copy(dz).start()
    tbown[...] = ytap[core * 4 + zlo] + tarcv[zlo]

    def place(r, y):
        for q in range(Q):
            sbuf[q, pl.ds(r, CTX, stride=16), :] = y[q * CTX:(q + 1) * CTX]

    for ch in range(8):
        g, h = spec[ch], hspec[ch]
        gr, gi, hr, hi = g[:, :R], g[:, R:], h[:, :R], h[:, R:]
        place(ch, inverse(gr * hr - gi * hi, gr * hi + gi * hr, e1q))
    for ch in range(8):
        d, h = spec[ch + 8], hspec[ch]
        dr, di, hr, hi = d[:, :R], d[:, R:], h[:, :R], h[:, R:]
        place(ch + 8, inverse(hr * dr + hi * di, hr * di - hi * dr, e1q))

    def narrow(c, _):
        rows = pl.ds(pl.multiple_of(c * 16, 16), 16)
        v = jnp.concatenate([sbuf[q, rows, :] for q in range(Q)], 1)
        osnd[c] = (v * SCALE).astype(BF16)
        return 0

    lax.fori_loop(0, CTX, narrow, 0)
    orcv[me] = osnd[me]

    def out_copy(i):
        c = peer(i)
        return remote(osnd.at[c], orcv.at[me], s_out.at[i], r_out.at[i], c, tp)

    others(lambda i: out_copy(i).start())

    for dz in (1, 2, 3):
        z_copy(dz).wait_recv()
    total = (tbown[...] + tbrcv[1].astype(F32) + tbrcv[2].astype(F32) + tbrcv[3].astype(F32)) * SCALE
    for c in range(CTX):
        csnd[c] = total[c * Q:(c + 1) * Q]
    crcv[me] = csnd[me]

    def c_copy(i):
        c = peer(i)
        return remote(csnd.at[c], crcv.at[me], s_c.at[i], r_c.at[i], c, tp)

    others(lambda i: c_copy(i).start())
    others(lambda i: c_copy(i).wait_recv())
    for c in range(CTX):
        cflat[c * Q:(c + 1) * Q, :] = crcv[c]
    dbuf[core, zlo] = jnp.concatenate([cflat[pl.ds(q, CTX, stride=Q), :] for q in range(Q)], 0).astype(BF16)

    def d_copy(dz):
        return remote(dbuf.at[core, zlo], dbuf.at[core, zlo], s_d.at[dz], r_d.at[dz], me, chip(dz))

    for dz in (1, 2, 3):
        d_copy(dz).start()
    for dz in (1, 2, 3):
        d_copy(dz).wait_recv()
    mate_d = remote(dbuf.at[core], dbuf.at[core], s_x.at[2], r_x.at[2], me, mate)
    mate_d.start()

    others(lambda i: out_copy(i).wait_recv())
    out_ref[...] = orcv[...]
    mate_d.wait_recv()
    fil_ref[...] = dbuf[...]

    others(lambda i: in_copy(i).wait_send())
    others(lambda i: f_copy(i).wait_send())
    others(lambda i: out_copy(i).wait_send())
    others(lambda i: c_copy(i).wait_send())
    for dz in (1, 2, 3):
        z_copy(dz).wait_send()
        d_copy(dz).wait_send()
    mate_f.wait_send()
    mate_t.wait_send()
    mate_d.wait_send()


def finish_kernel(o_ref, d_ref, c_ref, k_ref, v_ref, gq_ref, gk_ref, gv_ref, gf_ref, wide):
    def gates(j, _):
        rows = pl.ds(pl.multiple_of(j * 16, 16), 16)
        a, b = o_ref[2 * j].astype(F32), o_ref[2 * j + 1].astype(F32)
        conv = jnp.concatenate([a[:8], b[:8]], 0)
        grad = jnp.concatenate([a[8:], b[8:]], 0)
        gq_ref[rows, :] = (c_ref[rows, :].astype(F32) * conv).astype(BF16)
        gk_ref[rows, :] = (v_ref[rows, :].astype(F32) * grad).astype(BF16)
        gv_ref[rows, :] = (k_ref[rows, :].astype(F32) * grad).astype(BF16)
        return 0

    lax.fori_loop(0, CTX // 2, gates, 0)
    for f in range(8):
        v = d_ref[f // 4, f % 4].astype(F32)
        for q in range(Q):
            wide[q, pl.ds(f, CTX, stride=8), :] = v[q * CTX:(q + 1) * CTX]
    for q in range(Q):
        gf_ref[:, q * R:(q + 1) * R] = wide[q].astype(BF16)


def per_device(queries, key_branch, value_branch, filters, cotangent):
    vmem = pl.BlockSpec(memory_space=pltpu.VMEM)
    tabs = [jnp.asarray(t) for t in tables()]
    dma = pltpu.SemaphoreType.DMA
    out, fil = pl.pallas_call(
        exchange_kernel,
        out_shape=(
            jax.ShapeDtypeStruct((CTX, 16, TOK), BF16),
            jax.ShapeDtypeStruct((2, 4, R, R), BF16),
        ),
        in_specs=[vmem] * 11,
        out_specs=(vmem, vmem),
        scratch_shapes=[
            pltpu.VMEM((CTX, 16, TOK), BF16),
            pltpu.VMEM((CTX, 16, TOK), BF16),
            pltpu.VMEM((CTX, 16, TOK), BF16),
            pltpu.VMEM((CTX, 16, TOK), BF16),
            pltpu.VMEM((Q, 256, R), F32),
            pltpu.VMEM((CTX, 16, R), BF16),
            pltpu.VMEM((2, CTX, 16, R), BF16),
            pltpu.VMEM((Q, CTX * 16, R), F32),
            pltpu.VMEM((2, CTX * 16, R), F32),
            pltpu.VMEM((16, R, 2 * R), F32),
            pltpu.VMEM((8, R, 2 * R), F32),
            pltpu.VMEM((8, R, R), F32),
            pltpu.VMEM((4, R, R), F32),
            pltpu.VMEM((4, R, R), BF16),
            pltpu.VMEM((4, R, R), BF16),
            pltpu.VMEM((R, R), F32),
            pltpu.VMEM((CTX, Q, R), F32),
            pltpu.VMEM((CTX, Q, R), F32),
            pltpu.VMEM((R, R), F32),
            pltpu.VMEM((2, 4, R, R), BF16),
            dma((32,)), dma((32,)), dma((32,)), dma((32,)), dma((32,)), dma((32,)),
            dma((32,)), dma((32,)), dma((4,)), dma((4,)), dma((4,)), dma((4,)), dma((3,)), dma((3,)),
        ],
        compiler_params=pltpu.CompilerParams(
            collective_id=0, has_side_effects=True, vmem_limit_bytes=40 * 2**20),
        name="exchange",
    )(queries, key_branch, value_branch, filters, cotangent, *tabs)
    block = jax.ShapeDtypeStruct((256, TOK), BF16)
    return pl.pallas_call(
        finish_kernel,
        out_shape=(block,) * 4,
        in_specs=[vmem] * 5,
        out_specs=(vmem,) * 4,
        scratch_shapes=[pltpu.VMEM((Q, 256, R), F32)],
        compiler_params=pltpu.CompilerParams(vmem_limit_bytes=32 * 2**20),
        name="finish",
    )(out, fil, cotangent, key_branch, value_branch)


def solution(mesh):
    placed = (P("tp", "ctx"), P("tp", "ctx"), P("tp", "ctx"), P(None, "ctx"), P("tp", "ctx"))
    return jax.shard_map(
        per_device,
        mesh=mesh,
        in_specs=placed,
        out_specs=(P("tp", "ctx"), P("tp", "ctx"), P("tp", "ctx"), P(None, "ctx")),
        check_vma=False,
    )
```

```python
import jax
import jax.numpy as jnp
import ml_dtypes
import numpy as np
from jax import lax
from jax.experimental import pallas as pl
from jax.experimental.pallas import tpu as pltpu
from jax.sharding import PartitionSpec as P

MESH = pl.DeviceIdType.MESH
F32 = jnp.float32
BF16 = jnp.bfloat16

SEQ = 16384
FILTERS = 256
CTX = 32
TP = 8
TOK = SEQ // CTX
R = 128
Q = TOK // R
SCALE = 2.0**-21


def tables():
    k = np.arange(R, dtype=np.float64)[:, None]
    n = np.arange(R, dtype=np.float64)[None, :]
    angle = 2 * np.pi * (k + 0.25) * n / R
    outer = np.concatenate([np.cos(angle), -np.sin(angle)], 0)
    order = np.arange(R).reshape(CTX, Q).T.reshape(-1)
    twist = 2 * np.pi * (k + 0.25) * n / SEQ
    inner = 2 * np.pi * ((k * n) % R) / R
    c, s = np.cos(inner), np.sin(inner)
    fwd = np.block([[c, -s], [s, c]])
    as_bf16 = lambda t: np.asarray(t, np.float32).astype(ml_dtypes.bfloat16)
    return (
        as_bf16(outer[:, order]),
        np.stack([np.cos(twist), np.sin(twist)]).astype(np.float32),
        as_bf16(fwd),
        as_bf16(fwd.T),
        as_bf16(outer.T[order]),
        as_bf16(outer.T),
    )


def dot(a, b):
    return jnp.dot(a, b, preferred_element_type=F32)


def exchange_kernel(
    q_hbm, k_hbm, v_hbm, f_hbm, c_hbm, e1_hbm, tw_hbm, fw_hbm, fi_hbm, e1q_hbm, e1n_hbm,
    out_ref, fil_ref,
    q_ref, k_ref, v_ref, f_ref, c_ref, e1, tw, fw, fi, e1q, e1n, s_l,
    snd, rcv, osnd, orcv, fsnd, frcv, csnd, crcv,
    wide, fwide, fflat, win, wout, acc,
    s_in, r_in, s_f, r_f, s_out, r_out, s_c, r_c, s_x, r_x, s_own,
):
    me = lax.axis_index("ctx")
    tp = lax.axis_index("tp")
    core = tp % 2
    zlo = tp // 2
    mx, mz, my = me % 4, (me // 4) % 2, me // 8
    mine = me * TP + tp
    xs = [(mx + i) % 4 for i in range(4)]
    ys = [((my + i) % 4) * 8 for i in range(4)]
    zs = [mz * 4, (1 - mz) * 4]
    cs = [ys[j // 4] + xs[j % 4] + zs[1] for j in range(16)]
    cs += [ys[j // 4] + xs[j % 4] + zs[0] for j in range(1, 16)]
    all_cs = cs + [me]
    ts = [(tp + d) % TP for d in range(TP)]
    back = [(tp + TP - d) % TP for d in range(TP)]
    chips = [((zlo + d) % 4) * 2 + core for d in range(4)]
    mate = zlo * 2 + 1 - core

    def remote(src, dst, ss, rs, c, t):
        return pltpu.make_async_remote_copy(
            src_ref=src, dst_ref=dst, send_sem=ss, recv_sem=rs, device_id=(c, t), device_id_type=MESH)

    def drain(ref, sem):
        pltpu.make_async_copy(ref, ref, sem).wait()

    loads = [
        pltpu.make_async_copy(src, dst, s_l.at[i])
        for i, (src, dst) in enumerate((
            (k_hbm, k_ref), (v_hbm, v_ref), (c_hbm, c_ref), (q_hbm, q_ref), (f_hbm, f_ref), (e1_hbm, e1),
            (tw_hbm, tw), (fw_hbm, fw), (fi_hbm, fi), (e1q_hbm, e1q), (e1n_hbm, e1n)))
    ]
    for load in loads:
        load.start()

    barrier = pltpu.get_barrier_semaphore()
    for d in range(TP):
        for c in cs if d == 0 else all_cs:
            pl.semaphore_signal(barrier, inc=1, device_id=(c, ts[d]), device_id_type=MESH)

    for load in loads[:4]:
        load.wait()
    for q in range(Q):
        lanes = slice(q * R, (q + 1) * R)
        wide[pl.ds(q, FILTERS, stride=8), :] = k_ref[:, lanes].astype(F32) * v_ref[:, lanes].astype(F32)
        wide[pl.ds(Q + q, FILTERS, stride=8), :] = c_ref[:, lanes].astype(F32) * q_ref[:, lanes].astype(F32)
    snd[...] = wide[...].reshape(FILTERS, 8, R).astype(BF16)
    pl.semaphore_wait(barrier, CTX * TP - 1)

    def send_in(d):
        for c in cs if d == 0 else all_cs:
            remote(snd.at[c * TP + ts[d]], rcv.at[tp, me], s_in.at[0], r_in.at[d], c, ts[d]).start()

    own_in = pltpu.make_async_copy(snd.at[mine], rcv.at[tp, me], r_in.at[0])
    own_in.start()
    send_in(0)

    loads[4].wait()
    for q in range(Q):
        fwide[q] = f_ref[:, q * R:(q + 1) * R].astype(F32)
    for q in range(Q):
        fflat[pl.ds(q, CTX, stride=Q), :] = fwide[q, pl.ds(tp, CTX, stride=TP), :]
    for c in range(CTX):
        fsnd[c] = fflat[c * Q:(c + 1) * Q, :].astype(BF16)
    own_f = pltpu.make_async_copy(fsnd.at[me], frcv.at[me], r_f.at[0])
    own_f.start()
    for c in cs:
        remote(fsnd.at[c], frcv.at[me], s_f.at[0], r_f.at[0], c, tp).start()
    for d in range(1, TP):
        send_in(d)

    def forward(x):
        y = dot(e1[...], x)
        yr, yi = y[:R], y[R:]
        tc, ts_ = tw[0], tw[1]
        left = jnp.concatenate([(yr * tc + yi * ts_).astype(BF16), (yi * tc - yr * ts_).astype(BF16)], 1)
        z = dot(left, fw[...])
        return z[:, :R], z[:, R:]

    def inverse(pr, pi, out):
        u = dot(jnp.concatenate([pr.astype(BF16), pi.astype(BF16)], 1), fi[...])
        ur, ui = u[:, :R], u[:, R:]
        tc, ts_ = tw[0], tw[1]
        v = jnp.concatenate([(ur * tc - ui * ts_).astype(BF16), (ui * tc + ur * ts_).astype(BF16)], 0)
        return dot(out[...], v) * SCALE

    for load in loads[5:]:
        load.wait()
    hr = hi = None
    for d in range(TP):
        drain(rcv.at[back[d]], r_in.at[d])
        win[d] = rcv[back[d]].astype(F32).reshape(CTX * 8, R)
        x = jnp.concatenate([win[d, pl.ds(q, CTX, stride=8), :] for q in range(Q)], 0)
        gr, gi = forward(x.astype(BF16))
        x = jnp.concatenate([win[d, pl.ds(Q + q, CTX, stride=8), :] for q in range(Q)], 0)
        dr, di = forward(x.astype(BF16))
        if d == 0:
            acc[0] = gr * dr + gi * di
            acc[1] = gr * di - gi * dr
            drain(frcv, r_f.at[0])
            for c in range(CTX):
                fflat[c * Q:(c + 1) * Q, :] = frcv[c].astype(F32)
            x = jnp.concatenate([fflat[pl.ds(q, CTX, stride=Q), :] for q in range(Q)], 0)
            hr, hi = forward(x.astype(BF16))
        else:
            acc[0] += gr * dr + gi * di
            acc[1] += gr * di - gi * dr
        if d == TP - 1:
            total = inverse(acc[0], acc[1], e1n)
            for c in range(CTX):
                csnd[c] = total[c * Q:(c + 1) * Q].astype(BF16)
            pltpu.make_async_copy(csnd.at[me], crcv.at[core, me * 4 + zlo], r_c.at[0]).start()
            for z in range(4):
                for c in cs if z == 0 else all_cs:
                    remote(csnd.at[c], crcv.at[core, me * 4 + zlo], s_c.at[0], r_c.at[0], c, chips[z]).start()
        conv = inverse(gr * hr - gi * hi, gr * hi + gi * hr, e1q)
        grad = inverse(hr * dr + hi * di, hr * di - hi * dr, e1q)
        for q in range(Q):
            wout[d, pl.ds(q, CTX, stride=8), :] = conv[q * CTX:(q + 1) * CTX]
            wout[d, pl.ds(Q + q, CTX, stride=8), :] = grad[q * CTX:(q + 1) * CTX]
        osnd[d] = wout[d].reshape(CTX, 8, R).astype(BF16)
        if d == 0:
            pltpu.make_async_copy(osnd.at[0, me], orcv.at[mine], r_out.at[0]).start()
        for c in cs if d == 0 else all_cs:
            remote(osnd.at[d, c], orcv.at[mine], s_out.at[0], r_out.at[0], c, back[d]).start()

    drain(crcv.at[core], r_c.at[0])
    swap = remote(crcv.at[core], crcv.at[core], s_x.at[0], r_x.at[0], me, mate)
    swap.start()
    drain(orcv, r_out.at[0])
    out_ref[...] = orcv[...]
    swap.wait()
    fil_ref[...] = crcv[...]

    drain(snd.at[pl.ds(0, CTX * TP - 1)], s_in.at[0])
    drain(snd.at[pl.ds(0, CTX * TP - 1)], s_out.at[0])
    drain(fsnd.at[pl.ds(0, CTX - 1)], s_f.at[0])
    drain(crcv.at[0, pl.ds(0, CTX * 4 - 1)], s_c.at[0])


def finish_kernel(o_ref, d_ref, c_ref, k_ref, v_ref, gq_ref, gk_ref, gv_ref, gf_ref, wide, fflat, fwide):
    wide[...] = o_ref[...].astype(F32).reshape(FILTERS * 8, R)
    for q in range(Q):
        lanes = slice(q * R, (q + 1) * R)
        conv = wide[pl.ds(q, FILTERS, stride=8), :]
        grad = wide[pl.ds(Q + q, FILTERS, stride=8), :]
        gq_ref[:, lanes] = (c_ref[:, lanes].astype(F32) * conv).astype(BF16)
        gk_ref[:, lanes] = (v_ref[:, lanes].astype(F32) * grad).astype(BF16)
        gv_ref[:, lanes] = (k_ref[:, lanes].astype(F32) * grad).astype(BF16)
    for k in range(2):
        for i in range(CTX * 4):
            fflat[k, i * Q:(i + 1) * Q, :] = d_ref[k, i].astype(F32)
    for q in range(Q):
        for k in range(2):
            fwide[pl.ds(k, CTX * 4, stride=2), :] = fflat[k, pl.ds(q, CTX * 4, stride=Q), :]
        gf_ref[:, q * R:(q + 1) * R] = fwide[...].astype(BF16)


def per_device(queries, key_branch, value_branch, filters, cotangent):
    vmem = pl.BlockSpec(memory_space=pltpu.VMEM)
    tabs = [jnp.asarray(t) for t in tables()]
    dma = pltpu.SemaphoreType.DMA
    out, fil = pl.pallas_call(
        exchange_kernel,
        out_shape=(
            jax.ShapeDtypeStruct((FILTERS, 8, R), BF16),
            jax.ShapeDtypeStruct((2, CTX * 4, Q, R), BF16),
        ),
        in_specs=[pl.BlockSpec(memory_space=pltpu.HBM)] * 11,
        out_specs=(vmem, vmem),
        scratch_shapes=[pltpu.VMEM((256, TOK), BF16)] * 5
        + [pltpu.VMEM(t.shape, t.dtype) for t in tabs]
        + [
            dma((11,)),
            pltpu.VMEM((FILTERS, 8, R), BF16),
            pltpu.VMEM((TP, CTX, 8, R), BF16),
            pltpu.VMEM((TP, CTX, 8, R), BF16),
            pltpu.VMEM((FILTERS, 8, R), BF16),
            pltpu.VMEM((CTX, Q, R), BF16),
            pltpu.VMEM((CTX, Q, R), BF16),
            pltpu.VMEM((CTX, Q, R), BF16),
            pltpu.VMEM((2, CTX * 4, Q, R), BF16),
            pltpu.VMEM((FILTERS * 8, R), F32),
            pltpu.VMEM((Q, FILTERS, R), F32),
            pltpu.VMEM((CTX * Q, R), F32),
            pltpu.VMEM((TP, CTX * 8, R), F32),
            pltpu.VMEM((TP, CTX * 8, R), F32),
            pltpu.VMEM((2, R, R), F32),
            dma((1,)), dma((TP,)), dma((1,)), dma((1,)), dma((1,)), dma((1,)),
            dma((1,)), dma((1,)), dma((1,)), dma((1,)), dma((1,)),
        ],
        compiler_params=pltpu.CompilerParams(
            collective_id=0, has_side_effects=True, vmem_limit_bytes=40 * 2**20),
        name="exchange",
    )(*(pltpu.with_memory_space_constraint(a, pltpu.HBM)
        for a in (queries, key_branch, value_branch, filters, cotangent, *tabs)))
    block = jax.ShapeDtypeStruct((256, TOK), BF16)
    return pl.pallas_call(
        finish_kernel,
        out_shape=(block,) * 4,
        in_specs=[vmem] * 5,
        out_specs=(vmem,) * 4,
        scratch_shapes=[
            pltpu.VMEM((FILTERS * 8, R), F32),
            pltpu.VMEM((2, CTX * 4 * Q, R), F32),
            pltpu.VMEM((FILTERS, R), F32),
        ],
        compiler_params=pltpu.CompilerParams(vmem_limit_bytes=32 * 2**20),
        name="finish",
    )(out, fil, cotangent, key_branch, value_branch)


def solution(mesh):
    placed = (P("tp", "ctx"), P("tp", "ctx"), P("tp", "ctx"), P(None, "ctx"), P("tp", "ctx"))
    return jax.shard_map(
        per_device,
        mesh=mesh,
        in_specs=placed,
        out_specs=(P("tp", "ctx"), P("tp", "ctx"), P("tp", "ctx"), P(None, "ctx")),
        check_vma=False,
    )
```

```python
import jax
import jax.numpy as jnp
import ml_dtypes
import numpy as np
from jax import lax
from jax.experimental import pallas as pl
from jax.experimental.pallas import tpu as pltpu
from jax.sharding import PartitionSpec as P

MESH = pl.DeviceIdType.MESH
F32 = jnp.float32
BF16 = jnp.bfloat16

SEQ = 16384
FILTERS = 256
CTX = 32
TP = 8
TOK = SEQ // CTX
R = 128
Q = TOK // R
SCALE = 2.0**-21


def tables():
    k = np.arange(R, dtype=np.float64)[:, None]
    n = np.arange(R, dtype=np.float64)[None, :]
    angle = 2 * np.pi * (k + 0.25) * n / R
    outer = np.concatenate([np.cos(angle), -np.sin(angle)], 0)
    pair = np.zeros((2, 2 * R, CTX, 2, Q))
    pair[0, :, :, 0] = pair[1, :, :, 1] = outer.reshape(2 * R, CTX, Q)
    pair = pair.reshape(4 * R, 2 * R)
    twist = 2 * np.pi * (k + 0.25) * n / SEQ
    inner = 2 * np.pi * ((k * n) % R) / R
    c, s = np.cos(inner), np.sin(inner)
    fwd = np.block([[c, -s], [s, c]])
    as_bf16 = lambda t: np.asarray(t, np.float32).astype(ml_dtypes.bfloat16)
    return (
        as_bf16(pair),
        np.stack([np.cos(twist), np.sin(twist)]).astype(np.float32),
        as_bf16(fwd),
        as_bf16(fwd.T),
        as_bf16(pair.T),
        as_bf16(outer),
        as_bf16(outer.T),
    )


def dot(a, b):
    return jnp.dot(a, b, preferred_element_type=F32)


def exchange_kernel(
    q_hbm, k_hbm, v_hbm, f_hbm, c_hbm, e2_hbm, tw_hbm, fw_hbm, fi_hbm, e2t_hbm, e1_hbm, e1t_hbm,
    out_ref, fil_ref, k_ref, v_ref, c_ref,
    q_ref, f_ref, e2, tw, fw, fi, e2t, e1, e1t, s_l,
    snd, rcv, osnd, fsnd, frcv, csnd,
    wide, fwide, fflat, acc, spec,
    s_in, r_in, s_f, r_f, s_out, r_out, s_c, r_c, s_x, r_x, known,
):
    me = lax.axis_index("ctx")
    tp = lax.axis_index("tp")
    core = tp % 2
    zlo = tp // 2
    mx, mz, my = me % 4, (me // 4) % 2, me // 8
    mine = me * TP + tp
    xs = [(mx + i) % 4 for i in range(4)]
    ys = [((my + i) % 4) * 8 for i in range(4)]
    zs = [mz * 4, (1 - mz) * 4]
    xys = [ys[j // 4] + xs[j % 4] for j in range(16)]
    near = [xy + zs[0] for xy in xys]
    far = [xy + zs[1] for xy in xys]
    cs = far + near[1:]
    all_cs = cs + [me]

    def beside(dz, dk):
        return ((zlo + dz) % 4) * 2 + (core + dk) % 2

    sets = (((0, 0), (0, 1)), ((1, 0), (3, 0)), ((1, 1), (3, 1)), ((2, 0), (2, 1)))
    chips = [beside(dz, 0) for dz in (0, 1, 3, 2)]
    mate = beside(0, 1)

    def remote(src, dst, ss, rs, c, t):
        return pltpu.make_async_remote_copy(
            src_ref=src, dst_ref=dst, send_sem=ss, recv_sem=rs, device_id=(c, t), device_id_type=MESH)

    def drain(ref, sem):
        pltpu.make_async_copy(ref, ref, sem).wait()

    loads = [
        pltpu.make_async_copy(src, dst, s_l.at[i])
        for i, (src, dst) in enumerate((
            (k_hbm, k_ref), (v_hbm, v_ref), (c_hbm, c_ref), (q_hbm, q_ref), (f_hbm, f_ref), (e2_hbm, e2),
            (tw_hbm, tw), (fw_hbm, fw), (fi_hbm, fi), (e2t_hbm, e2t), (e1_hbm, e1), (e1t_hbm, e1t)))
    ]
    for load in loads[:4]:
        load.start()

    barrier = pltpu.get_barrier_semaphore()
    for c in cs:
        for t in (tp, mate):
            pl.semaphore_signal(barrier, inc=1, device_id=(c, t), device_id_type=MESH)
    for t in (mate, *chips[1:]):
        pl.semaphore_signal(barrier, inc=1, device_id=(me, t), device_id_type=MESH)
    for load in loads[4:]:
        load.start()

    for load in loads[:4]:
        load.wait()
    for q in range(Q):
        lanes = slice(q * R, (q + 1) * R)
        wide[pl.ds(q, FILTERS, stride=8), :] = k_ref[:, lanes].astype(F32) * v_ref[:, lanes].astype(F32)
        wide[pl.ds(Q + q, FILTERS, stride=8), :] = c_ref[:, lanes].astype(F32) * q_ref[:, lanes].astype(F32)
    snd[...] = wide[...].reshape(FILTERS, 8, R).astype(BF16)
    pl.semaphore_wait(barrier, 2 * CTX - 1 + 3)
    for t in chips[1:]:
        pl.semaphore_signal(known, inc=1, device_id=(me, t), device_id_type=MESH)

    def send_in(n):
        for c in all_cs:
            for i, (dz, dk) in enumerate(sets[n]):
                if c is not me or dz or dk:
                    t = beside(dz, dk)
                    remote(snd.at[c * TP + t], rcv.at[tp, me], s_in.at[0], r_in.at[n, i], c, t).start()

    pltpu.make_async_copy(snd.at[mine], rcv.at[tp, me], r_in.at[0, 0]).start()
    send_in(0)

    loads[4].wait()
    for q in range(Q):
        fwide[q] = f_ref[:, q * R:(q + 1) * R].astype(F32)
    for q in range(Q):
        fflat[pl.ds(q, CTX, stride=Q), :] = fwide[q, pl.ds(tp, CTX, stride=TP), :]
    fsnd[...] = fflat[...].astype(BF16).reshape(CTX, Q, R)
    own_f = pltpu.make_async_copy(fsnd.at[me], frcv.at[me], r_f.at[0])
    own_f.start()
    for c in cs:
        remote(fsnd.at[c], frcv.at[me], s_f.at[0], r_f.at[0], c, tp).start()
    pl.semaphore_wait(known, 3)
    for n in range(1, 4):
        send_in(n)

    def twist(y):
        yr, yi = y[:R], y[R:]
        tc, ts_ = tw[0], tw[1]
        return jnp.concatenate([(yr * tc + yi * ts_).astype(BF16), (yi * tc - yr * ts_).astype(BF16)], 1)

    def untwist(u):
        ur, ui = u[:, :R], u[:, R:]
        tc, ts_ = tw[0], tw[1]
        return jnp.concatenate([(ur * tc - ui * ts_).astype(BF16), (ui * tc + ur * ts_).astype(BF16)], 0)

    def pack(pr, pi):
        return jnp.concatenate([pr.astype(BF16), pi.astype(BF16)], 1)

    for load in loads[5:]:
        load.wait()
    def sources(n):
        return [beside(4 - dz, dk) for dz, dk in sets[n]]

    def analyse(n):
        left = []
        for i, t in enumerate(sources(n)):
            drain(rcv.at[t], r_in.at[n, i])
        for i, t in enumerate(sources(n)):
            y = dot(e2[...], rcv[t].reshape(CTX * 8, R))
            left += [twist(y[:2 * R]), twist(y[2 * R:])]
        z = dot(jnp.concatenate(left, 0), fw[...])
        for i in range(2):
            g, d = z[2 * i * R:(2 * i + 1) * R], z[(2 * i + 1) * R:(2 * i + 2) * R]
            gr, gi, dr, di = g[:, :R], g[:, R:], d[:, :R], d[:, R:]
            sr, si = gr * dr + gi * di, gr * di - gi * dr
            if n == 0 and i == 0:
                acc[0], acc[1] = sr, si
            else:
                acc[0] += sr
                acc[1] += si
            spec[2 * n + i, 0], spec[2 * n + i, 1], spec[2 * n + i, 2], spec[2 * n + i, 3] = gr, gi, dr, di

    def results(n):
        hr, hi = acc[2], acc[3]
        parts = []
        for i in range(2):
            gr, gi, dr, di = (spec[2 * n + i, j] for j in range(4))
            parts += [pack(gr * hr - gi * hi, gr * hi + gi * hr), pack(hr * dr + hi * di, hr * di - hi * dr)]
        u = dot(jnp.concatenate(parts, 0), fi[...])
        for i in range(2):
            v = [untwist(u[j * R:(j + 1) * R]) for j in (2 * i, 2 * i + 1)]
            y = dot(e2t[...], jnp.concatenate(v, 0)) * SCALE
            osnd[2 * n + i] = y.astype(BF16).reshape(CTX, 8, R)
        if n == 0:
            pltpu.make_async_copy(osnd.at[0, me], out_ref.at[mine], r_out.at[0]).start()
        for c in all_cs:
            for i, t in enumerate(sources(n)):
                if c is not me or n or i:
                    remote(osnd.at[2 * n + i, c], out_ref.at[mine], s_out.at[0], r_out.at[0], c, t).start()

    def filter_gradient():
        u = dot(pack(acc[0], acc[1]), fi[...])
        total = dot(e1t[...], untwist(u)) * SCALE
        csnd[...] = total.astype(BF16).reshape(CTX, Q, R)
        place = fil_ref.at[core, me * 4 + zlo]
        pltpu.make_async_copy(csnd.at[me], place, r_c.at[0]).start()
        for c in all_cs:
            for i, t in enumerate(chips):
                if c is not me or i:
                    remote(csnd.at[c], place, s_c.at[0], r_c.at[0], c, t).start()

    analyse(0)
    drain(frcv, r_f.at[0])
    h = dot(twist(dot(e1[...], frcv[...].reshape(CTX * Q, R))), fw[...])
    acc[2], acc[3] = h[:, :R], h[:, R:]
    results(0)
    analyse(1)
    results(1)
    analyse(2)
    results(2)
    analyse(3)
    filter_gradient()
    results(3)

    drain(fil_ref.at[core], r_c.at[0])
    swap = remote(fil_ref.at[core], fil_ref.at[core], s_x.at[0], r_x.at[0], me, mate)
    swap.start()
    drain(out_ref, r_out.at[0])
    swap.wait()

    drain(snd.at[pl.ds(0, CTX * TP - 1)], s_in.at[0])
    drain(snd.at[pl.ds(0, CTX * TP - 1)], s_out.at[0])
    drain(fsnd.at[pl.ds(0, CTX - 1)], s_f.at[0])
    drain(fil_ref.at[0, pl.ds(0, CTX * 4 - 1)], s_c.at[0])


def finish_kernel(o_ref, d_ref, c_ref, k_ref, v_ref, gq_ref, gk_ref, gv_ref, gf_ref, wide, fflat, fwide):
    wide[...] = o_ref[...].astype(F32).reshape(FILTERS * 8, R)
    for q in range(Q):
        lanes = slice(q * R, (q + 1) * R)
        conv = wide[pl.ds(q, FILTERS, stride=8), :]
        grad = wide[pl.ds(Q + q, FILTERS, stride=8), :]
        gq_ref[:, lanes] = (c_ref[:, lanes].astype(F32) * conv).astype(BF16)
        gk_ref[:, lanes] = (v_ref[:, lanes].astype(F32) * grad).astype(BF16)
        gv_ref[:, lanes] = (k_ref[:, lanes].astype(F32) * grad).astype(BF16)
    fflat[...] = d_ref[...].astype(F32).reshape(2, CTX * 4 * Q, R)
    for q in range(Q):
        for k in range(2):
            fwide[pl.ds(k, CTX * 4, stride=2), :] = fflat[k, pl.ds(q, CTX * 4, stride=Q), :]
        gf_ref[:, q * R:(q + 1) * R] = fwide[...].astype(BF16)


def per_device(queries, key_branch, value_branch, filters, cotangent):
    vmem = pl.BlockSpec(memory_space=pltpu.VMEM)
    tabs = [jnp.asarray(t) for t in tables()]
    dma = pltpu.SemaphoreType.DMA
    block = jax.ShapeDtypeStruct((256, TOK), BF16)
    out, fil, key, value, cot = pl.pallas_call(
        exchange_kernel,
        out_shape=(
            jax.ShapeDtypeStruct((FILTERS, 8, R), BF16),
            jax.ShapeDtypeStruct((2, CTX * 4, Q, R), BF16),
            block, block, block,
        ),
        in_specs=[pl.BlockSpec(memory_space=pltpu.HBM)] * 12,
        out_specs=(vmem,) * 5,
        scratch_shapes=[pltpu.VMEM((256, TOK), BF16)] * 2
        + [pltpu.VMEM(t.shape, t.dtype) for t in tabs]
        + [
            dma((12,)),
            pltpu.VMEM((FILTERS, 8, R), BF16),
            pltpu.VMEM((TP, CTX, 8, R), BF16),
            pltpu.VMEM((TP, CTX, 8, R), BF16),
            pltpu.VMEM((CTX, Q, R), BF16),
            pltpu.VMEM((CTX, Q, R), BF16),
            pltpu.VMEM((CTX, Q, R), BF16),
            pltpu.VMEM((FILTERS * 8, R), F32),
            pltpu.VMEM((Q, FILTERS, R), F32),
            pltpu.VMEM((CTX * Q, R), F32),
            pltpu.VMEM((4, R, R), F32),
            pltpu.VMEM((TP, 4, R, R), F32),
            dma((1,)), dma((4, 2)), dma((1,)), dma((1,)), dma((1,)), dma((1,)),
            dma((1,)), dma((1,)), dma((1,)), dma((1,)), pltpu.SemaphoreType.REGULAR,
        ],
        compiler_params=pltpu.CompilerParams(
            collective_id=0, has_side_effects=True, vmem_limit_bytes=40 * 2**20),
        name="exchange",
    )(*(pltpu.with_memory_space_constraint(a, pltpu.HBM)
        for a in (queries, key_branch, value_branch, filters, cotangent, *tabs)))
    return pl.pallas_call(
        finish_kernel,
        out_shape=(block,) * 4,
        in_specs=[vmem] * 5,
        out_specs=(vmem,) * 4,
        scratch_shapes=[
            pltpu.VMEM((FILTERS * 8, R), F32),
            pltpu.VMEM((2, CTX * 4 * Q, R), F32),
            pltpu.VMEM((FILTERS, R), F32),
        ],
        compiler_params=pltpu.CompilerParams(vmem_limit_bytes=32 * 2**20),
        name="finish",
    )(out, fil, cot, key, value)


def solution(mesh):
    placed = (P("tp", "ctx"), P("tp", "ctx"), P("tp", "ctx"), P(None, "ctx"), P("tp", "ctx"))
    return jax.shard_map(
        per_device,
        mesh=mesh,
        in_specs=placed,
        out_specs=(P("tp", "ctx"), P("tp", "ctx"), P("tp", "ctx"), P(None, "ctx")),
        check_vma=False,
    )
```

```python
import jax
import jax.numpy as jnp
import ml_dtypes
import numpy as np
from jax import lax
from jax.experimental import pallas as pl
from jax.experimental.pallas import tpu as pltpu
from jax.sharding import PartitionSpec as P

MESH = pl.DeviceIdType.MESH
F32 = jnp.float32
BF16 = jnp.bfloat16

SEQ = 16384
FILTERS = 256
CTX = 32
TP = 8
TOK = SEQ // CTX
R = 128
Q = TOK // R
SCALE = 2.0**-21


def tables():
    k = np.arange(R, dtype=np.float64)[:, None]
    n = np.arange(R, dtype=np.float64)[None, :]
    angle = 2 * np.pi * (k + 0.25) * n / R
    outer = np.concatenate([np.cos(angle), -np.sin(angle)], 0)
    pair = np.zeros((2, 2 * R, CTX, 2, Q))
    pair[0, :, :, 0] = pair[1, :, :, 1] = outer.reshape(2 * R, CTX, Q)
    pair = pair.reshape(4 * R, 2 * R)
    twist = 2 * np.pi * (k + 0.25) * n / SEQ
    inner = 2 * np.pi * ((k * n) % R) / R
    c, s = np.cos(inner), np.sin(inner)
    fwd = np.block([[c, -s], [s, c]])
    as_bf16 = lambda t: np.asarray(t, np.float32).astype(ml_dtypes.bfloat16)
    return (
        as_bf16(pair),
        np.stack([np.cos(twist), np.sin(twist)]).astype(np.float32),
        as_bf16(fwd),
        as_bf16(fwd.T),
        as_bf16(pair.T),
        as_bf16(outer),
        as_bf16(outer.T),
    )


def dot(a, b):
    return jnp.dot(a, b, preferred_element_type=F32)


def exchange_kernel(
    q_hbm, k_hbm, v_hbm, f_hbm, c_hbm, e2_hbm, tw_hbm, fw_hbm, fi_hbm, e2t_hbm, e1_hbm, e1t_hbm,
    out_ref, fil_ref, k_ref, v_ref, c_ref,
    q_ref, f_ref, e2, tw, fw, fi, e2t, e1, e1t, s_l,
    snd, rcv, osnd, fsnd, frcv, csnd,
    wide, fwide, fflat, acc, spec,
    s_in, r_in, s_f, r_f, s_out, r_out, s_c, r_c, s_x, r_x, known,
):
    me = lax.axis_index("ctx")
    tp = lax.axis_index("tp")
    core = tp % 2
    zlo = tp // 2
    mx, mz, my = me % 4, (me // 4) % 2, me // 8
    mine = me * TP + tp
    xs = [(mx + i) % 4 for i in range(4)]
    ys = [((my + i) % 4) * 8 for i in range(4)]
    zs = [mz * 4, (1 - mz) * 4]
    xys = [ys[j // 4] + xs[j % 4] for j in range(16)]
    near = [xy + zs[0] for xy in xys]
    far = [xy + zs[1] for xy in xys]
    cs = far + near[1:]
    all_cs = cs + [me]

    def beside(dz, dk):
        return ((zlo + dz) % 4) * 2 + (core + dk) % 2

    sets = (((0, 0), (0, 1)), ((2, 0), (2, 1)), ((1, 0), (3, 0)), ((1, 1), (3, 1)))
    chips = [beside(dz, 0) for dz in (0, 1, 3, 2)]
    mate = beside(0, 1)

    def remote(src, dst, ss, rs, c, t):
        return pltpu.make_async_remote_copy(
            src_ref=src, dst_ref=dst, send_sem=ss, recv_sem=rs, device_id=(c, t), device_id_type=MESH)

    def drain(ref, sem):
        pltpu.make_async_copy(ref, ref, sem).wait()

    loads = [
        pltpu.make_async_copy(src, dst, s_l.at[i])
        for i, (src, dst) in enumerate((
            (k_hbm, k_ref), (v_hbm, v_ref), (c_hbm, c_ref), (q_hbm, q_ref), (f_hbm, f_ref), (e2_hbm, e2),
            (tw_hbm, tw), (fw_hbm, fw), (fi_hbm, fi), (e2t_hbm, e2t), (e1_hbm, e1), (e1t_hbm, e1t)))
    ]
    for load in loads[:4]:
        load.start()

    barrier = pltpu.get_barrier_semaphore()
    for c in cs:
        for t in (tp, mate):
            pl.semaphore_signal(barrier, inc=1, device_id=(c, t), device_id_type=MESH)
    for t in (mate, *chips[1:]):
        pl.semaphore_signal(barrier, inc=1, device_id=(me, t), device_id_type=MESH)
    for load in loads[4:]:
        load.start()

    for load in loads[:4]:
        load.wait()
    for q in range(Q):
        lanes = slice(q * R, (q + 1) * R)
        wide[pl.ds(q, FILTERS, stride=8), :] = k_ref[:, lanes].astype(F32) * v_ref[:, lanes].astype(F32)
        wide[pl.ds(Q + q, FILTERS, stride=8), :] = c_ref[:, lanes].astype(F32) * q_ref[:, lanes].astype(F32)
    snd[...] = wide[...].reshape(FILTERS, 8, R).astype(BF16)
    pl.semaphore_wait(barrier, 2 * CTX - 1 + 3)
    for t in chips[1:]:
        pl.semaphore_signal(known, inc=1, device_id=(me, t), device_id_type=MESH)

    def send_in(n):
        for c in all_cs:
            for i, (dz, dk) in enumerate(sets[n]):
                if c is not me or dz or dk:
                    t = beside(dz, dk)
                    remote(snd.at[c * TP + t], rcv.at[tp, me], s_in.at[0], r_in.at[n, i], c, t).start()

    pltpu.make_async_copy(snd.at[mine], rcv.at[tp, me], r_in.at[0, 0]).start()
    send_in(0)

    loads[4].wait()
    for q in range(Q):
        fwide[q] = f_ref[:, q * R:(q + 1) * R].astype(F32)
    for q in range(Q):
        fflat[pl.ds(q, CTX, stride=Q), :] = fwide[q, pl.ds(tp, CTX, stride=TP), :]
    fsnd[...] = fflat[...].astype(BF16).reshape(CTX, Q, R)
    own_f = pltpu.make_async_copy(fsnd.at[me], frcv.at[me], r_f.at[0])
    own_f.start()
    for c in cs:
        remote(fsnd.at[c], frcv.at[me], s_f.at[0], r_f.at[0], c, tp).start()
    pl.semaphore_wait(known, 3)
    for n in range(1, 4):
        send_in(n)

    def twist(y):
        yr, yi = y[:R], y[R:]
        tc, ts_ = tw[0], tw[1]
        return jnp.concatenate([(yr * tc + yi * ts_).astype(BF16), (yi * tc - yr * ts_).astype(BF16)], 1)

    def untwist(u):
        ur, ui = u[:, :R], u[:, R:]
        tc, ts_ = tw[0], tw[1]
        return jnp.concatenate([(ur * tc - ui * ts_).astype(BF16), (ui * tc + ur * ts_).astype(BF16)], 0)

    def pack(pr, pi):
        return jnp.concatenate([pr.astype(BF16), pi.astype(BF16)], 1)

    for load in loads[5:]:
        load.wait()
    def sources(n):
        return [beside(4 - dz, dk) for dz, dk in sets[n]]

    def analyse(n):
        left = []
        for i, t in enumerate(sources(n)):
            drain(rcv.at[t], r_in.at[n, i])
        for i, t in enumerate(sources(n)):
            y = dot(e2[...], rcv[t].reshape(CTX * 8, R))
            left += [twist(y[:2 * R]), twist(y[2 * R:])]
        z = dot(jnp.concatenate(left, 0), fw[...])
        for i in range(2):
            g, d = z[2 * i * R:(2 * i + 1) * R], z[(2 * i + 1) * R:(2 * i + 2) * R]
            gr, gi, dr, di = g[:, :R], g[:, R:], d[:, :R], d[:, R:]
            sr, si = gr * dr + gi * di, gr * di - gi * dr
            if n == 0 and i == 0:
                acc[0], acc[1] = sr, si
            else:
                acc[0] += sr
                acc[1] += si
            spec[2 * n + i, 0], spec[2 * n + i, 1], spec[2 * n + i, 2], spec[2 * n + i, 3] = gr, gi, dr, di

    def results(n):
        hr, hi = acc[2], acc[3]
        parts = []
        for i in range(2):
            gr, gi, dr, di = (spec[2 * n + i, j] for j in range(4))
            parts += [pack(gr * hr - gi * hi, gr * hi + gi * hr), pack(hr * dr + hi * di, hr * di - hi * dr)]
        u = dot(jnp.concatenate(parts, 0), fi[...])
        for i in range(2):
            v = [untwist(u[j * R:(j + 1) * R]) for j in (2 * i, 2 * i + 1)]
            y = dot(e2t[...], jnp.concatenate(v, 0)) * SCALE
            osnd[2 * n + i] = y.astype(BF16).reshape(CTX, 8, R)
        if n == 0:
            pltpu.make_async_copy(osnd.at[0, me], out_ref.at[mine], r_out.at[0]).start()
        for c in all_cs:
            for i, t in enumerate(sources(n)):
                if c is not me or n or i:
                    remote(osnd.at[2 * n + i, c], out_ref.at[mine], s_out.at[0], r_out.at[0], c, t).start()

    def filter_gradient():
        u = dot(pack(acc[0], acc[1]), fi[...])
        total = dot(e1t[...], untwist(u)) * SCALE
        csnd[...] = total.astype(BF16).reshape(CTX, Q, R)
        place = fil_ref.at[core, me * 4 + zlo]
        pltpu.make_async_copy(csnd.at[me], place, r_c.at[0]).start()
        for c in all_cs:
            for i, t in enumerate(chips):
                if c is not me or i:
                    remote(csnd.at[c], place, s_c.at[0], r_c.at[0], c, t).start()

    analyse(0)
    drain(frcv, r_f.at[0])
    h = dot(twist(dot(e1[...], frcv[...].reshape(CTX * Q, R))), fw[...])
    acc[2], acc[3] = h[:, :R], h[:, R:]
    results(0)
    analyse(1)
    results(1)
    analyse(2)
    results(2)
    analyse(3)
    filter_gradient()
    results(3)

    drain(fil_ref.at[core], r_c.at[0])
    swap = remote(fil_ref.at[core], fil_ref.at[core], s_x.at[0], r_x.at[0], me, mate)
    swap.start()
    drain(out_ref, r_out.at[0])
    swap.wait()

    drain(snd.at[pl.ds(0, CTX * TP - 1)], s_in.at[0])
    drain(snd.at[pl.ds(0, CTX * TP - 1)], s_out.at[0])
    drain(fsnd.at[pl.ds(0, CTX - 1)], s_f.at[0])
    drain(fil_ref.at[0, pl.ds(0, CTX * 4 - 1)], s_c.at[0])


def finish_kernel(o_ref, d_ref, c_ref, k_ref, v_ref, gq_ref, gk_ref, gv_ref, gf_ref, wide, fflat, fwide):
    wide[...] = o_ref[...].astype(F32).reshape(FILTERS * 8, R)
    for q in range(Q):
        lanes = slice(q * R, (q + 1) * R)
        conv = wide[pl.ds(q, FILTERS, stride=8), :]
        grad = wide[pl.ds(Q + q, FILTERS, stride=8), :]
        gq_ref[:, lanes] = (c_ref[:, lanes].astype(F32) * conv).astype(BF16)
        gk_ref[:, lanes] = (v_ref[:, lanes].astype(F32) * grad).astype(BF16)
        gv_ref[:, lanes] = (k_ref[:, lanes].astype(F32) * grad).astype(BF16)
    fflat[...] = d_ref[...].astype(F32).reshape(2, CTX * 4 * Q, R)
    for q in range(Q):
        for k in range(2):
            fwide[pl.ds(k, CTX * 4, stride=2), :] = fflat[k, pl.ds(q, CTX * 4, stride=Q), :]
        gf_ref[:, q * R:(q + 1) * R] = fwide[...].astype(BF16)


def per_device(queries, key_branch, value_branch, filters, cotangent):
    vmem = pl.BlockSpec(memory_space=pltpu.VMEM)
    tabs = [jnp.asarray(t) for t in tables()]
    dma = pltpu.SemaphoreType.DMA
    block = jax.ShapeDtypeStruct((256, TOK), BF16)
    out, fil, key, value, cot = pl.pallas_call(
        exchange_kernel,
        out_shape=(
            jax.ShapeDtypeStruct((FILTERS, 8, R), BF16),
            jax.ShapeDtypeStruct((2, CTX * 4, Q, R), BF16),
            block, block, block,
        ),
        in_specs=[pl.BlockSpec(memory_space=pltpu.HBM)] * 12,
        out_specs=(vmem,) * 5,
        scratch_shapes=[pltpu.VMEM((256, TOK), BF16)] * 2
        + [pltpu.VMEM(t.shape, t.dtype) for t in tabs]
        + [
            dma((12,)),
            pltpu.VMEM((FILTERS, 8, R), BF16),
            pltpu.VMEM((TP, CTX, 8, R), BF16),
            pltpu.VMEM((TP, CTX, 8, R), BF16),
            pltpu.VMEM((CTX, Q, R), BF16),
            pltpu.VMEM((CTX, Q, R), BF16),
            pltpu.VMEM((CTX, Q, R), BF16),
            pltpu.VMEM((FILTERS * 8, R), F32),
            pltpu.VMEM((Q, FILTERS, R), F32),
            pltpu.VMEM((CTX * Q, R), F32),
            pltpu.VMEM((4, R, R), F32),
            pltpu.VMEM((TP, 4, R, R), F32),
            dma((1,)), dma((4, 2)), dma((1,)), dma((1,)), dma((1,)), dma((1,)),
            dma((1,)), dma((1,)), dma((1,)), dma((1,)), pltpu.SemaphoreType.REGULAR,
        ],
        compiler_params=pltpu.CompilerParams(
            collective_id=0, has_side_effects=True, vmem_limit_bytes=40 * 2**20),
        name="exchange",
    )(*(pltpu.with_memory_space_constraint(a, pltpu.HBM)
        for a in (queries, key_branch, value_branch, filters, cotangent, *tabs)))
    return pl.pallas_call(
        finish_kernel,
        out_shape=(block,) * 4,
        in_specs=[vmem] * 5,
        out_specs=(vmem,) * 4,
        scratch_shapes=[
            pltpu.VMEM((FILTERS * 8, R), F32),
            pltpu.VMEM((2, CTX * 4 * Q, R), F32),
            pltpu.VMEM((FILTERS, R), F32),
        ],
        compiler_params=pltpu.CompilerParams(vmem_limit_bytes=32 * 2**20),
        name="finish",
    )(out, fil, cot, key, value)


def solution(mesh):
    placed = (P("tp", "ctx"), P("tp", "ctx"), P("tp", "ctx"), P(None, "ctx"), P("tp", "ctx"))
    return jax.shard_map(
        per_device,
        mesh=mesh,
        in_specs=placed,
        out_specs=(P("tp", "ctx"), P("tp", "ctx"), P("tp", "ctx"), P(None, "ctx")),
        check_vma=False,
    )
```

```python
import jax
import jax.numpy as jnp
import ml_dtypes
import numpy as np
from jax import lax
from jax.experimental import pallas as pl
from jax.experimental.pallas import tpu as pltpu
from jax.sharding import PartitionSpec as P

MESH = pl.DeviceIdType.MESH
F32 = jnp.float32
BF16 = jnp.bfloat16

SEQ = 16384
FILTERS = 256
CTX = 32
TP = 8
TOK = SEQ // CTX
R = 128
Q = TOK // R
SCALE = 2.0**-21


def tables():
    k = np.arange(R, dtype=np.float64)[:, None]
    n = np.arange(R, dtype=np.float64)[None, :]
    angle = 2 * np.pi * (k + 0.25) * n / R
    outer = np.concatenate([np.cos(angle), -np.sin(angle)], 0)
    pair = np.zeros((2, 2 * R, CTX, 2, Q))
    pair[0, :, :, 0] = pair[1, :, :, 1] = outer.reshape(2 * R, CTX, Q)
    pair = pair.reshape(4 * R, 2 * R)
    twist = 2 * np.pi * (k + 0.25) * n / SEQ
    inner = 2 * np.pi * ((k * n) % R) / R
    c, s = np.cos(inner), np.sin(inner)
    fwd = np.block([[c, -s], [s, c]])
    as_bf16 = lambda t: np.asarray(t, np.float32).astype(ml_dtypes.bfloat16)
    return (
        as_bf16(pair),
        np.stack([np.cos(twist), np.sin(twist)]).astype(np.float32),
        as_bf16(fwd),
        as_bf16(fwd.T),
        as_bf16(pair.T),
        as_bf16(outer),
        as_bf16(outer.T),
    )


def dot(a, b):
    return jnp.dot(a, b, preferred_element_type=F32)


def exchange_kernel(
    q_hbm, k_hbm, v_hbm, f_hbm, c_hbm, e2_hbm, tw_hbm, fw_hbm, fi_hbm, e2t_hbm, e1_hbm, e1t_hbm,
    out_ref, fil_ref, k_ref, v_ref, c_ref,
    q_ref, f_ref, e2, tw, fw, fi, e2t, e1, e1t, s_l,
    snd, rcv, osnd, fsnd, frcv, csnd,
    wide, fwide, fflat, acc, spec,
    s_in, r_in, s_f, r_f, s_out, r_out, s_c, r_c, s_x, r_x, known,
):
    me = lax.axis_index("ctx")
    tp = lax.axis_index("tp")
    core = tp % 2
    zlo = tp // 2
    mx, mz, my = me % 4, (me // 4) % 2, me // 8
    mine = me * TP + tp
    xs = [(mx + i) % 4 for i in range(4)]
    ys = [((my + i) % 4) * 8 for i in range(4)]
    zs = [mz * 4, (1 - mz) * 4]
    xys = [ys[j // 4] + xs[j % 4] for j in range(16)]
    near = [xy + zs[0] for xy in xys]
    far = [xy + zs[1] for xy in xys]
    cs = far + near[1:]
    all_cs = cs + [me]

    def beside(dz, dk):
        return ((zlo + dz) % 4) * 2 + (core + dk) % 2

    sets = (((0, 0), (0, 1)), ((2, 0), (2, 1)), ((1, 0), (3, 0)), ((1, 1), (3, 1)))
    chips = [beside(dz, 0) for dz in (0, 1, 3, 2)]
    mate = beside(0, 1)

    def remote(src, dst, ss, rs, c, t):
        return pltpu.make_async_remote_copy(
            src_ref=src, dst_ref=dst, send_sem=ss, recv_sem=rs, device_id=(c, t), device_id_type=MESH)

    def drain(ref, sem):
        pltpu.make_async_copy(ref, ref, sem).wait()

    loads = [
        pltpu.make_async_copy(src, dst, s_l.at[i])
        for i, (src, dst) in enumerate((
            (k_hbm, k_ref), (v_hbm, v_ref), (c_hbm, c_ref), (q_hbm, q_ref), (f_hbm, f_ref), (e2_hbm, e2),
            (tw_hbm, tw), (fw_hbm, fw), (fi_hbm, fi), (e2t_hbm, e2t), (e1_hbm, e1), (e1t_hbm, e1t)))
    ]
    for load in loads[:4]:
        load.start()

    barrier = pltpu.get_barrier_semaphore()
    for c in cs:
        for t in (tp, mate):
            pl.semaphore_signal(barrier, inc=1, device_id=(c, t), device_id_type=MESH)
    for t in (mate, *chips[1:]):
        pl.semaphore_signal(barrier, inc=1, device_id=(me, t), device_id_type=MESH)
    for load in loads[4:]:
        load.start()

    for load in loads[:4]:
        load.wait()
    for q in range(Q):
        lanes = slice(q * R, (q + 1) * R)
        wide[pl.ds(q, FILTERS, stride=8), :] = k_ref[:, lanes].astype(F32) * v_ref[:, lanes].astype(F32)
        wide[pl.ds(Q + q, FILTERS, stride=8), :] = c_ref[:, lanes].astype(F32) * q_ref[:, lanes].astype(F32)
    snd[...] = wide[...].reshape(FILTERS, 8, R).astype(BF16)
    pl.semaphore_wait(barrier, 2 * CTX - 1 + 3)
    for t in chips[1:]:
        pl.semaphore_signal(known, inc=1, device_id=(me, t), device_id_type=MESH)

    def send_in(n):
        for c in all_cs:
            for i, (dz, dk) in enumerate(sets[n]):
                if c is not me or dz or dk:
                    t = beside(dz, dk)
                    remote(snd.at[c * TP + t], rcv.at[tp, me], s_in.at[0], r_in.at[n, i], c, t).start()

    pltpu.make_async_copy(snd.at[mine], rcv.at[tp, me], r_in.at[0, 0]).start()
    send_in(0)

    loads[4].wait()
    for q in range(Q):
        fwide[q] = f_ref[:, q * R:(q + 1) * R].astype(F32)
    for q in range(Q):
        fflat[pl.ds(q, CTX, stride=Q), :] = fwide[q, pl.ds(tp, CTX, stride=TP), :]
    fsnd[...] = fflat[...].astype(BF16).reshape(CTX, Q, R)
    own_f = pltpu.make_async_copy(fsnd.at[me], frcv.at[me], r_f.at[0])
    own_f.start()
    for c in cs:
        remote(fsnd.at[c], frcv.at[me], s_f.at[0], r_f.at[0], c, tp).start()
    pl.semaphore_wait(known, 3)
    for n in range(1, 4):
        send_in(n)

    def twist(y):
        yr, yi = y[:R], y[R:]
        tc, ts_ = tw[0], tw[1]
        return jnp.concatenate([(yr * tc + yi * ts_).astype(BF16), (yi * tc - yr * ts_).astype(BF16)], 1)

    def untwist(u):
        ur, ui = u[:, :R], u[:, R:]
        tc, ts_ = tw[0], tw[1]
        return jnp.concatenate([(ur * tc - ui * ts_).astype(BF16), (ui * tc + ur * ts_).astype(BF16)], 0)

    def pack(pr, pi):
        return jnp.concatenate([pr.astype(BF16), pi.astype(BF16)], 1)

    for load in loads[5:]:
        load.wait()
    def sources(n):
        return [beside(4 - dz, dk) for dz, dk in sets[n]]

    def analyse(n):
        left = []
        for i, t in enumerate(sources(n)):
            drain(rcv.at[t], r_in.at[n, i])
        for i, t in enumerate(sources(n)):
            y = dot(e2[...], rcv[t].reshape(CTX * 8, R))
            left += [twist(y[:2 * R]), twist(y[2 * R:])]
        z = dot(jnp.concatenate(left, 0), fw[...])
        for i in range(2):
            g, d = z[2 * i * R:(2 * i + 1) * R], z[(2 * i + 1) * R:(2 * i + 2) * R]
            gr, gi, dr, di = g[:, :R], g[:, R:], d[:, :R], d[:, R:]
            sr, si = gr * dr + gi * di, gr * di - gi * dr
            if n == 0 and i == 0:
                acc[0], acc[1] = sr, si
            else:
                acc[0] += sr
                acc[1] += si
            spec[2 * n + i, 0], spec[2 * n + i, 1], spec[2 * n + i, 2], spec[2 * n + i, 3] = gr, gi, dr, di

    def halves(kinds, send):
        for h in range(2):
            for x, y in sorted(((x, y) for y in range(4) for x in range(4)), key=lambda p: min(p[0], 2) + min(p[1], 2)):
                for kind in kinds:
                    c = y * 8 + h * 4 + x
                    if kind:
                        send(c, kind)
                    else:
                        pl.when(me != c)(lambda c=c, kind=kind: send(c, kind))

    def results(n):
        hr, hi = acc[2], acc[3]
        parts = []
        for i in range(2):
            gr, gi, dr, di = (spec[2 * n + i, j] for j in range(4))
            parts += [pack(gr * hr - gi * hi, gr * hi + gi * hr), pack(hr * dr + hi * di, hr * di - hi * dr)]
        u = dot(jnp.concatenate(parts, 0), fi[...])
        for i in range(2):
            v = [untwist(u[j * R:(j + 1) * R]) for j in (2 * i, 2 * i + 1)]
            y = dot(e2t[...], jnp.concatenate(v, 0)) * SCALE
            osnd[2 * n + i] = y.astype(BF16).reshape(CTX, 8, R)
        if n == 0:
            pltpu.make_async_copy(osnd.at[0, me], out_ref.at[mine], r_out.at[0]).start()
        def send(c, kind):
            i = kind - 2 * n
            remote(osnd.at[kind, c], out_ref.at[mine], s_out.at[0], r_out.at[0], c, sources(n)[i]).start()

        halves((2 * n, 2 * n + 1), send)

    def filter_gradient():
        u = dot(pack(acc[0], acc[1]), fi[...])
        total = dot(e1t[...], untwist(u)) * SCALE
        csnd[...] = total.astype(BF16).reshape(CTX, Q, R)
        place = fil_ref.at[core, me * 4 + zlo]
        pltpu.make_async_copy(csnd.at[me], place, r_c.at[0]).start()
        halves(range(4), lambda c, i: remote(csnd.at[c], place, s_c.at[0], r_c.at[0], c, chips[i]).start())

    analyse(0)
    drain(frcv, r_f.at[0])
    h = dot(twist(dot(e1[...], frcv[...].reshape(CTX * Q, R))), fw[...])
    acc[2], acc[3] = h[:, :R], h[:, R:]
    results(0)
    analyse(1)
    results(1)
    analyse(2)
    results(2)
    analyse(3)
    filter_gradient()
    results(3)

    drain(fil_ref.at[core], r_c.at[0])
    swap = remote(fil_ref.at[core], fil_ref.at[core], s_x.at[0], r_x.at[0], me, mate)
    swap.start()
    drain(out_ref, r_out.at[0])
    swap.wait()

    drain(snd.at[pl.ds(0, CTX * TP - 1)], s_in.at[0])
    drain(snd.at[pl.ds(0, CTX * TP - 1)], s_out.at[0])
    drain(fsnd.at[pl.ds(0, CTX - 1)], s_f.at[0])
    drain(fil_ref.at[0, pl.ds(0, CTX * 4 - 1)], s_c.at[0])


def finish_kernel(o_ref, d_ref, c_ref, k_ref, v_ref, gq_ref, gk_ref, gv_ref, gf_ref, wide, fflat, fwide):
    wide[...] = o_ref[...].astype(F32).reshape(FILTERS * 8, R)
    for q in range(Q):
        lanes = slice(q * R, (q + 1) * R)
        conv = wide[pl.ds(q, FILTERS, stride=8), :]
        grad = wide[pl.ds(Q + q, FILTERS, stride=8), :]
        gq_ref[:, lanes] = (c_ref[:, lanes].astype(F32) * conv).astype(BF16)
        gk_ref[:, lanes] = (v_ref[:, lanes].astype(F32) * grad).astype(BF16)
        gv_ref[:, lanes] = (k_ref[:, lanes].astype(F32) * grad).astype(BF16)
    fflat[...] = d_ref[...].astype(F32).reshape(2, CTX * 4 * Q, R)
    for q in range(Q):
        for k in range(2):
            fwide[pl.ds(k, CTX * 4, stride=2), :] = fflat[k, pl.ds(q, CTX * 4, stride=Q), :]
        gf_ref[:, q * R:(q + 1) * R] = fwide[...].astype(BF16)


def per_device(queries, key_branch, value_branch, filters, cotangent):
    vmem = pl.BlockSpec(memory_space=pltpu.VMEM)
    tabs = [jnp.asarray(t) for t in tables()]
    dma = pltpu.SemaphoreType.DMA
    block = jax.ShapeDtypeStruct((256, TOK), BF16)
    out, fil, key, value, cot = pl.pallas_call(
        exchange_kernel,
        out_shape=(
            jax.ShapeDtypeStruct((FILTERS, 8, R), BF16),
            jax.ShapeDtypeStruct((2, CTX * 4, Q, R), BF16),
            block, block, block,
        ),
        in_specs=[pl.BlockSpec(memory_space=pltpu.HBM)] * 12,
        out_specs=(vmem,) * 5,
        scratch_shapes=[pltpu.VMEM((256, TOK), BF16)] * 2
        + [pltpu.VMEM(t.shape, t.dtype) for t in tabs]
        + [
            dma((12,)),
            pltpu.VMEM((FILTERS, 8, R), BF16),
            pltpu.VMEM((TP, CTX, 8, R), BF16),
            pltpu.VMEM((TP, CTX, 8, R), BF16),
            pltpu.VMEM((CTX, Q, R), BF16),
            pltpu.VMEM((CTX, Q, R), BF16),
            pltpu.VMEM((CTX, Q, R), BF16),
            pltpu.VMEM((FILTERS * 8, R), F32),
            pltpu.VMEM((Q, FILTERS, R), F32),
            pltpu.VMEM((CTX * Q, R), F32),
            pltpu.VMEM((4, R, R), F32),
            pltpu.VMEM((TP, 4, R, R), F32),
            dma((1,)), dma((4, 2)), dma((1,)), dma((1,)), dma((1,)), dma((1,)),
            dma((1,)), dma((1,)), dma((1,)), dma((1,)), pltpu.SemaphoreType.REGULAR,
        ],
        compiler_params=pltpu.CompilerParams(
            collective_id=0, has_side_effects=True, vmem_limit_bytes=40 * 2**20),
        name="exchange",
    )(*(pltpu.with_memory_space_constraint(a, pltpu.HBM)
        for a in (queries, key_branch, value_branch, filters, cotangent, *tabs)))
    return pl.pallas_call(
        finish_kernel,
        out_shape=(block,) * 4,
        in_specs=[vmem] * 5,
        out_specs=(vmem,) * 4,
        scratch_shapes=[
            pltpu.VMEM((FILTERS * 8, R), F32),
            pltpu.VMEM((2, CTX * 4 * Q, R), F32),
            pltpu.VMEM((FILTERS, R), F32),
        ],
        compiler_params=pltpu.CompilerParams(vmem_limit_bytes=32 * 2**20),
        name="finish",
    )(out, fil, cot, key, value)


def solution(mesh):
    placed = (P("tp", "ctx"), P("tp", "ctx"), P("tp", "ctx"), P(None, "ctx"), P("tp", "ctx"))
    return jax.shard_map(
        per_device,
        mesh=mesh,
        in_specs=placed,
        out_specs=(P("tp", "ctx"), P("tp", "ctx"), P("tp", "ctx"), P(None, "ctx")),
        check_vma=False,
    )
```

```python
import jax
import jax.numpy as jnp
import ml_dtypes
import numpy as np
from jax import lax
from jax.experimental import pallas as pl
from jax.experimental.pallas import tpu as pltpu
from jax.sharding import PartitionSpec as P

MESH = pl.DeviceIdType.MESH
F32 = jnp.float32
BF16 = jnp.bfloat16

SEQ = 16384
FILTERS = 256
CTX = 32
TP = 8
TOK = SEQ // CTX
R = 128
Q = TOK // R
SCALE = 2.0**-21


def tables():
    k = np.arange(R, dtype=np.float64)[:, None]
    n = np.arange(R, dtype=np.float64)[None, :]
    angle = 2 * np.pi * (k + 0.25) * n / R
    outer = np.concatenate([np.cos(angle), -np.sin(angle)], 0)
    pair = np.zeros((2, 2 * R, CTX, 2, Q))
    pair[0, :, :, 0] = pair[1, :, :, 1] = outer.reshape(2 * R, CTX, Q)
    pair = pair.reshape(4 * R, 2 * R)
    twist = 2 * np.pi * (k + 0.25) * n / SEQ
    inner = 2 * np.pi * ((k * n) % R) / R
    c, s = np.cos(inner), np.sin(inner)
    fwd = np.block([[c, -s], [s, c]])
    as_bf16 = lambda t: np.asarray(t, np.float32).astype(ml_dtypes.bfloat16)
    return (
        as_bf16(pair),
        np.stack([np.cos(twist), np.sin(twist)]).astype(np.float32),
        as_bf16(fwd),
        as_bf16(fwd.T),
        as_bf16(pair.T),
        as_bf16(outer),
        as_bf16(outer.T),
    )


def dot(a, b):
    return jnp.dot(a, b, preferred_element_type=F32)


def exchange_kernel(
    q_hbm, k_hbm, v_hbm, f_hbm, c_hbm, e2_hbm, tw_hbm, fw_hbm, fi_hbm, e2t_hbm, e1_hbm, e1t_hbm,
    out_ref, fil_ref, k_ref, v_ref, c_ref,
    q_ref, f_ref, e2, tw, fw, fi, e2t, e1, e1t, s_l,
    snd, rcv, osnd, fsnd, frcv, csnd,
    wide, fwide, fflat, acc, spec,
    s_in, r_in, s_f, r_f, s_out, r_out, s_c, r_c, s_x, r_x, known,
):
    me = lax.axis_index("ctx")
    tp = lax.axis_index("tp")
    core = tp % 2
    zlo = tp // 2
    mx, mz, my = me % 4, (me // 4) % 2, me // 8
    mine = me * TP + tp
    xs = [(mx + i) % 4 for i in range(4)]
    ys = [((my + i) % 4) * 8 for i in range(4)]
    zs = [mz * 4, (1 - mz) * 4]
    xys = [ys[j // 4] + xs[j % 4] for j in range(16)]
    near = [xy + zs[0] for xy in xys]
    far = [xy + zs[1] for xy in xys]
    cs = far + near[1:]
    all_cs = cs + [me]

    def beside(dz, dk):
        return ((zlo + dz) % 4) * 2 + (core + dk) % 2

    sets = (((0, 0), (0, 1)), ((2, 0), (2, 1)), ((1, 0), (3, 0)), ((1, 1), (3, 1)))
    chips = [beside(dz, 0) for dz in (0, 1, 3, 2)]
    mate = beside(0, 1)

    def remote(src, dst, ss, rs, c, t):
        return pltpu.make_async_remote_copy(
            src_ref=src, dst_ref=dst, send_sem=ss, recv_sem=rs, device_id=(c, t), device_id_type=MESH)

    def drain(ref, sem):
        pltpu.make_async_copy(ref, ref, sem).wait()

    loads = [
        pltpu.make_async_copy(src, dst, s_l.at[i])
        for i, (src, dst) in enumerate((
            (k_hbm, k_ref), (v_hbm, v_ref), (c_hbm, c_ref), (q_hbm, q_ref), (f_hbm, f_ref), (e2_hbm, e2),
            (tw_hbm, tw), (fw_hbm, fw), (fi_hbm, fi), (e2t_hbm, e2t), (e1_hbm, e1), (e1t_hbm, e1t)))
    ]
    for load in loads[:4]:
        load.start()

    barrier = pltpu.get_barrier_semaphore()
    for c in cs:
        for t in (tp, mate):
            pl.semaphore_signal(barrier, inc=1, device_id=(c, t), device_id_type=MESH)
    for t in (mate, *chips[1:]):
        pl.semaphore_signal(barrier, inc=1, device_id=(me, t), device_id_type=MESH)
    for load in loads[4:]:
        load.start()

    for load in loads[:4]:
        load.wait()
    for q in range(Q):
        lanes = slice(q * R, (q + 1) * R)
        wide[pl.ds(q, FILTERS, stride=8), :] = k_ref[:, lanes].astype(F32) * v_ref[:, lanes].astype(F32)
        wide[pl.ds(Q + q, FILTERS, stride=8), :] = c_ref[:, lanes].astype(F32) * q_ref[:, lanes].astype(F32)
    snd[...] = wide[...].reshape(FILTERS, 8, R).astype(BF16)
    pl.semaphore_wait(barrier, 2 * CTX - 1 + 3)
    for t in chips[1:]:
        pl.semaphore_signal(known, inc=1, device_id=(me, t), device_id_type=MESH)

    late = sorted((y * 8 + x for y in range(4) for x in range(4)), key=lambda p: -min(p % 8, 2) - min(p // 8, 2))

    def send_in(n):
        for h in (1, 0):
            for j in range(16):
                for i, (dz, dk) in enumerate(sets[n]):
                    t = beside(dz, dk)
                    c = late[j] + 4 * h if n > 0 else (far if h else near)[j]

                    def send(c=c, t=t, i=i):
                        remote(snd.at[c * TP + t], rcv.at[tp, me], s_in.at[0], r_in.at[n, i], c, t).start()

                    if j or dz or dk:
                        send()
                    elif h:
                        send()

    pltpu.make_async_copy(snd.at[mine], rcv.at[tp, me], r_in.at[0, 0]).start()
    send_in(0)

    loads[4].wait()
    for q in range(Q):
        fwide[q] = f_ref[:, q * R:(q + 1) * R].astype(F32)
    for q in range(Q):
        fflat[pl.ds(q, CTX, stride=Q), :] = fwide[q, pl.ds(tp, CTX, stride=TP), :]
    fsnd[...] = fflat[...].astype(BF16).reshape(CTX, Q, R)
    own_f = pltpu.make_async_copy(fsnd.at[me], frcv.at[me], r_f.at[0])
    own_f.start()
    for c in cs:
        remote(fsnd.at[c], frcv.at[me], s_f.at[0], r_f.at[0], c, tp).start()
    pl.semaphore_wait(known, 3)
    for n in range(1, 4):
        send_in(n)

    def twist(y):
        yr, yi = y[:R], y[R:]
        tc, ts_ = tw[0], tw[1]
        return jnp.concatenate([(yr * tc + yi * ts_).astype(BF16), (yi * tc - yr * ts_).astype(BF16)], 1)

    def untwist(u):
        ur, ui = u[:, :R], u[:, R:]
        tc, ts_ = tw[0], tw[1]
        return jnp.concatenate([(ur * tc - ui * ts_).astype(BF16), (ui * tc + ur * ts_).astype(BF16)], 0)

    def pack(pr, pi):
        return jnp.concatenate([pr.astype(BF16), pi.astype(BF16)], 1)

    for load in loads[5:]:
        load.wait()
    def sources(n):
        return [beside(4 - dz, dk) for dz, dk in sets[n]]

    def analyse(n):
        left = []
        for i, t in enumerate(sources(n)):
            drain(rcv.at[t], r_in.at[n, i])
        for i, t in enumerate(sources(n)):
            y = dot(e2[...], rcv[t].reshape(CTX * 8, R))
            left += [twist(y[:2 * R]), twist(y[2 * R:])]
        z = dot(jnp.concatenate(left, 0), fw[...])
        for i in range(2):
            g, d = z[2 * i * R:(2 * i + 1) * R], z[(2 * i + 1) * R:(2 * i + 2) * R]
            gr, gi, dr, di = g[:, :R], g[:, R:], d[:, :R], d[:, R:]
            sr, si = gr * dr + gi * di, gr * di - gi * dr
            if n == 0 and i == 0:
                acc[0], acc[1] = sr, si
            else:
                acc[0] += sr
                acc[1] += si
            spec[2 * n + i, 0], spec[2 * n + i, 1], spec[2 * n + i, 2], spec[2 * n + i, 3] = gr, gi, dr, di

    def halves(kinds, send):
        for h in range(2):
            for x, y in sorted(((x, y) for y in range(4) for x in range(4)), key=lambda p: min(p[0], 2) + min(p[1], 2)):
                for kind in kinds:
                    c = y * 8 + h * 4 + x
                    if kind:
                        send(c, kind)
                    else:
                        pl.when(me != c)(lambda c=c, kind=kind: send(c, kind))

    def results(n):
        hr, hi = acc[2], acc[3]
        parts = []
        for i in range(2):
            gr, gi, dr, di = (spec[2 * n + i, j] for j in range(4))
            parts += [pack(gr * hr - gi * hi, gr * hi + gi * hr), pack(hr * dr + hi * di, hr * di - hi * dr)]
        u = dot(jnp.concatenate(parts, 0), fi[...])
        for i in range(2):
            v = [untwist(u[j * R:(j + 1) * R]) for j in (2 * i, 2 * i + 1)]
            y = dot(e2t[...], jnp.concatenate(v, 0)) * SCALE
            osnd[2 * n + i] = y.astype(BF16).reshape(CTX, 8, R)
        if n == 0:
            pltpu.make_async_copy(osnd.at[0, me], out_ref.at[mine], r_out.at[0]).start()
        def send(c, kind):
            i = kind - 2 * n
            remote(osnd.at[kind, c], out_ref.at[mine], s_out.at[0], r_out.at[0], c, sources(n)[i]).start()

        halves((2 * n, 2 * n + 1), send)

    def filter_gradient():
        u = dot(pack(acc[0], acc[1]), fi[...])
        total = dot(e1t[...], untwist(u)) * SCALE
        csnd[...] = total.astype(BF16).reshape(CTX, Q, R)
        place = fil_ref.at[core, me * 4 + zlo]
        pltpu.make_async_copy(csnd.at[me], place, r_c.at[0]).start()
        halves(range(4), lambda c, i: remote(csnd.at[c], place, s_c.at[0], r_c.at[0], c, chips[i]).start())

    analyse(0)
    drain(frcv, r_f.at[0])
    h = dot(twist(dot(e1[...], frcv[...].reshape(CTX * Q, R))), fw[...])
    acc[2], acc[3] = h[:, :R], h[:, R:]
    results(0)
    analyse(1)
    results(1)
    analyse(2)
    results(2)
    analyse(3)
    filter_gradient()
    results(3)

    drain(fil_ref.at[core], r_c.at[0])
    swap = remote(fil_ref.at[core], fil_ref.at[core], s_x.at[0], r_x.at[0], me, mate)
    swap.start()
    drain(out_ref, r_out.at[0])
    swap.wait()

    drain(snd.at[pl.ds(0, CTX * TP - 1)], s_in.at[0])
    drain(snd.at[pl.ds(0, CTX * TP - 1)], s_out.at[0])
    drain(fsnd.at[pl.ds(0, CTX - 1)], s_f.at[0])
    drain(fil_ref.at[0, pl.ds(0, CTX * 4 - 1)], s_c.at[0])


def finish_kernel(o_ref, d_ref, c_ref, k_ref, v_ref, gq_ref, gk_ref, gv_ref, gf_ref, wide, fflat, fwide):
    wide[...] = o_ref[...].astype(F32).reshape(FILTERS * 8, R)
    for q in range(Q):
        lanes = slice(q * R, (q + 1) * R)
        conv = wide[pl.ds(q, FILTERS, stride=8), :]
        grad = wide[pl.ds(Q + q, FILTERS, stride=8), :]
        gq_ref[:, lanes] = (c_ref[:, lanes].astype(F32) * conv).astype(BF16)
        gk_ref[:, lanes] = (v_ref[:, lanes].astype(F32) * grad).astype(BF16)
        gv_ref[:, lanes] = (k_ref[:, lanes].astype(F32) * grad).astype(BF16)
    fflat[...] = d_ref[...].astype(F32).reshape(2, CTX * 4 * Q, R)
    for q in range(Q):
        for k in range(2):
            fwide[pl.ds(k, CTX * 4, stride=2), :] = fflat[k, pl.ds(q, CTX * 4, stride=Q), :]
        gf_ref[:, q * R:(q + 1) * R] = fwide[...].astype(BF16)


def per_device(queries, key_branch, value_branch, filters, cotangent):
    vmem = pl.BlockSpec(memory_space=pltpu.VMEM)
    tabs = [jnp.asarray(t) for t in tables()]
    dma = pltpu.SemaphoreType.DMA
    block = jax.ShapeDtypeStruct((256, TOK), BF16)
    out, fil, key, value, cot = pl.pallas_call(
        exchange_kernel,
        out_shape=(
            jax.ShapeDtypeStruct((FILTERS, 8, R), BF16),
            jax.ShapeDtypeStruct((2, CTX * 4, Q, R), BF16),
            block, block, block,
        ),
        in_specs=[pl.BlockSpec(memory_space=pltpu.HBM)] * 12,
        out_specs=(vmem,) * 5,
        scratch_shapes=[pltpu.VMEM((256, TOK), BF16)] * 2
        + [pltpu.VMEM(t.shape, t.dtype) for t in tabs]
        + [
            dma((12,)),
            pltpu.VMEM((FILTERS, 8, R), BF16),
            pltpu.VMEM((TP, CTX, 8, R), BF16),
            pltpu.VMEM((TP, CTX, 8, R), BF16),
            pltpu.VMEM((CTX, Q, R), BF16),
            pltpu.VMEM((CTX, Q, R), BF16),
            pltpu.VMEM((CTX, Q, R), BF16),
            pltpu.VMEM((FILTERS * 8, R), F32),
            pltpu.VMEM((Q, FILTERS, R), F32),
            pltpu.VMEM((CTX * Q, R), F32),
            pltpu.VMEM((4, R, R), F32),
            pltpu.VMEM((TP, 4, R, R), F32),
            dma((1,)), dma((4, 2)), dma((1,)), dma((1,)), dma((1,)), dma((1,)),
            dma((1,)), dma((1,)), dma((1,)), dma((1,)), pltpu.SemaphoreType.REGULAR,
        ],
        compiler_params=pltpu.CompilerParams(
            collective_id=0, has_side_effects=True, vmem_limit_bytes=40 * 2**20),
        name="exchange",
    )(*(pltpu.with_memory_space_constraint(a, pltpu.HBM)
        for a in (queries, key_branch, value_branch, filters, cotangent, *tabs)))
    return pl.pallas_call(
        finish_kernel,
        out_shape=(block,) * 4,
        in_specs=[vmem] * 5,
        out_specs=(vmem,) * 4,
        scratch_shapes=[
            pltpu.VMEM((FILTERS * 8, R), F32),
            pltpu.VMEM((2, CTX * 4 * Q, R), F32),
            pltpu.VMEM((FILTERS, R), F32),
        ],
        compiler_params=pltpu.CompilerParams(vmem_limit_bytes=32 * 2**20),
        name="finish",
    )(out, fil, cot, key, value)


def solution(mesh):
    placed = (P("tp", "ctx"), P("tp", "ctx"), P("tp", "ctx"), P(None, "ctx"), P("tp", "ctx"))
    return jax.shard_map(
        per_device,
        mesh=mesh,
        in_specs=placed,
        out_specs=(P("tp", "ctx"), P("tp", "ctx"), P("tp", "ctx"), P(None, "ctx")),
        check_vma=False,
    )
```

```python
import jax
import jax.numpy as jnp
import ml_dtypes
import numpy as np
from jax import lax
from jax.experimental import pallas as pl
from jax.experimental.pallas import tpu as pltpu
from jax.sharding import PartitionSpec as P

MESH = pl.DeviceIdType.MESH
F32 = jnp.float32
BF16 = jnp.bfloat16

SEQ = 16384
FILTERS = 256
CTX = 32
TP = 8
TOK = SEQ // CTX
R = 128
Q = TOK // R
SCALE = 2.0**-21


def tables():
    k = np.arange(R, dtype=np.float64)[:, None]
    n = np.arange(R, dtype=np.float64)[None, :]
    angle = 2 * np.pi * (k + 0.25) * n / R
    outer = np.concatenate([np.cos(angle), -np.sin(angle)], 0)
    pair = np.zeros((2, 2 * R, CTX, 2, Q))
    pair[0, :, :, 0] = pair[1, :, :, 1] = outer.reshape(2 * R, CTX, Q)
    pair = pair.reshape(4 * R, 2 * R)
    twist = 2 * np.pi * (k + 0.25) * n / SEQ
    inner = 2 * np.pi * ((k * n) % R) / R
    c, s = np.cos(inner), np.sin(inner)
    fwd = np.block([[c, -s], [s, c]])
    as_bf16 = lambda t: np.asarray(t, np.float32).astype(ml_dtypes.bfloat16)
    return (
        as_bf16(pair),
        np.stack([np.cos(twist), np.sin(twist)]).astype(np.float32),
        as_bf16(fwd),
        as_bf16(fwd.T),
        as_bf16(pair.T),
        as_bf16(outer),
        as_bf16(outer.T),
    )


def dot(a, b):
    return jnp.dot(a, b, preferred_element_type=F32)


def exchange_kernel(
    q_hbm, k_hbm, v_hbm, f_hbm, c_hbm, e2_hbm, tw_hbm, fw_hbm, fi_hbm, e2t_hbm, e1_hbm, e1t_hbm,
    out_ref, fil_ref, k_ref, v_ref, c_ref,
    q_ref, f_ref, e2, tw, fw, fi, e2t, e1, e1t, s_l,
    snd, rcv, osnd, fsnd, frcv, csnd,
    wide, fwide, fflat, acc, spec,
    s_in, r_in, s_f, r_f, s_out, r_out, s_c, r_c, s_x, r_x, known,
):
    me = lax.axis_index("ctx")
    tp = lax.axis_index("tp")
    core = tp % 2
    zlo = tp // 2
    mx, mz, my = me % 4, (me // 4) % 2, me // 8
    mine = me * TP + tp
    xs = [(mx + i) % 4 for i in range(4)]
    ys = [((my + i) % 4) * 8 for i in range(4)]
    zs = [mz * 4, (1 - mz) * 4]
    xys = [ys[j // 4] + xs[j % 4] for j in range(16)]
    near = [xy + zs[0] for xy in xys]
    far = [xy + zs[1] for xy in xys]
    cs = far + near[1:]
    all_cs = cs + [me]

    def beside(dz, dk):
        return ((zlo + dz) % 4) * 2 + (core + dk) % 2

    sets = (((0, 0), (0, 1)), ((2, 0), (2, 1)), ((1, 0), (3, 0)), ((1, 1), (3, 1)))
    chips = [beside(dz, 0) for dz in (0, 1, 3, 2)]
    mate = beside(0, 1)

    def remote(src, dst, ss, rs, c, t):
        return pltpu.make_async_remote_copy(
            src_ref=src, dst_ref=dst, send_sem=ss, recv_sem=rs, device_id=(c, t), device_id_type=MESH)

    def drain(ref, sem):
        pltpu.make_async_copy(ref, ref, sem).wait()

    loads = [
        pltpu.make_async_copy(src, dst, s_l.at[i])
        for i, (src, dst) in enumerate((
            (k_hbm, k_ref), (v_hbm, v_ref), (c_hbm, c_ref), (q_hbm, q_ref), (f_hbm, f_ref), (e2_hbm, e2),
            (tw_hbm, tw), (fw_hbm, fw), (fi_hbm, fi), (e2t_hbm, e2t), (e1_hbm, e1), (e1t_hbm, e1t)))
    ]
    for load in loads[:4]:
        load.start()

    barrier = pltpu.get_barrier_semaphore()
    for c in cs:
        for t in (tp, mate):
            pl.semaphore_signal(barrier, inc=1, device_id=(c, t), device_id_type=MESH)
    for t in (mate, *chips[1:]):
        pl.semaphore_signal(barrier, inc=1, device_id=(me, t), device_id_type=MESH)
    for load in loads[4:]:
        load.start()

    for load in loads[:4]:
        load.wait()
    for q in range(Q):
        lanes = slice(q * R, (q + 1) * R)
        wide[pl.ds(q, FILTERS, stride=8), :] = k_ref[:, lanes].astype(F32) * v_ref[:, lanes].astype(F32)
        wide[pl.ds(Q + q, FILTERS, stride=8), :] = c_ref[:, lanes].astype(F32) * q_ref[:, lanes].astype(F32)
    snd[...] = wide[...].reshape(FILTERS, 8, R).astype(BF16)
    pl.semaphore_wait(barrier, 2 * CTX - 1 + 3)
    for t in chips[1:]:
        pl.semaphore_signal(known, inc=1, device_id=(me, t), device_id_type=MESH)

    late = sorted((y * 8 + x for y in range(4) for x in range(4)), key=lambda p: -min(p % 8, 2) - min(p // 8, 2))

    def send_in(n):
        for h in (1, 0):
            for j in range(16):
                for i, (dz, dk) in enumerate(sets[n]):
                    t = beside(dz, dk)
                    c = late[j] + 4 * h if n > 0 else (late[j] + zs[1] if h else near[j])

                    def send(c=c, t=t, i=i):
                        remote(snd.at[c * TP + t], rcv.at[tp, me], s_in.at[0], r_in.at[n, i], c, t).start()

                    if j or dz or dk:
                        send()
                    elif h:
                        send()

    pltpu.make_async_copy(snd.at[mine], rcv.at[tp, me], r_in.at[0, 0]).start()
    send_in(0)

    loads[4].wait()
    for q in range(Q):
        fwide[q] = f_ref[:, q * R:(q + 1) * R].astype(F32)
    for q in range(Q):
        fflat[pl.ds(q, CTX, stride=Q), :] = fwide[q, pl.ds(tp, CTX, stride=TP), :]
    fsnd[...] = fflat[...].astype(BF16).reshape(CTX, Q, R)
    own_f = pltpu.make_async_copy(fsnd.at[me], frcv.at[me], r_f.at[0])
    own_f.start()
    for c in cs:
        remote(fsnd.at[c], frcv.at[me], s_f.at[0], r_f.at[0], c, tp).start()
    pl.semaphore_wait(known, 3)
    for n in range(1, 4):
        send_in(n)

    def twist(y):
        yr, yi = y[:R], y[R:]
        tc, ts_ = tw[0], tw[1]
        return jnp.concatenate([(yr * tc + yi * ts_).astype(BF16), (yi * tc - yr * ts_).astype(BF16)], 1)

    def untwist(u):
        ur, ui = u[:, :R], u[:, R:]
        tc, ts_ = tw[0], tw[1]
        return jnp.concatenate([(ur * tc - ui * ts_).astype(BF16), (ui * tc + ur * ts_).astype(BF16)], 0)

    def pack(pr, pi):
        return jnp.concatenate([pr.astype(BF16), pi.astype(BF16)], 1)

    for load in loads[5:]:
        load.wait()
    def sources(n):
        return [beside(4 - dz, dk) for dz, dk in sets[n]]

    def analyse(n):
        left = []
        for i, t in enumerate(sources(n)):
            drain(rcv.at[t], r_in.at[n, i])
        for i, t in enumerate(sources(n)):
            y = dot(e2[...], rcv[t].reshape(CTX * 8, R))
            left += [twist(y[:2 * R]), twist(y[2 * R:])]
        z = dot(jnp.concatenate(left, 0), fw[...])
        for i in range(2):
            g, d = z[2 * i * R:(2 * i + 1) * R], z[(2 * i + 1) * R:(2 * i + 2) * R]
            gr, gi, dr, di = g[:, :R], g[:, R:], d[:, :R], d[:, R:]
            sr, si = gr * dr + gi * di, gr * di - gi * dr
            if n == 0 and i == 0:
                acc[0], acc[1] = sr, si
            else:
                acc[0] += sr
                acc[1] += si
            spec[2 * n + i, 0], spec[2 * n + i, 1], spec[2 * n + i, 2], spec[2 * n + i, 3] = gr, gi, dr, di

    def halves(kinds, send):
        for h in range(2):
            for x, y in sorted(((x, y) for y in range(4) for x in range(4)), key=lambda p: min(p[0], 2) + min(p[1], 2)):
                for kind in kinds:
                    c = y * 8 + h * 4 + x
                    if kind:
                        send(c, kind)
                    else:
                        pl.when(me != c)(lambda c=c, kind=kind: send(c, kind))

    def results(n):
        hr, hi = acc[2], acc[3]
        parts = []
        for i in range(2):
            gr, gi, dr, di = (spec[2 * n + i, j] for j in range(4))
            parts += [pack(gr * hr - gi * hi, gr * hi + gi * hr), pack(hr * dr + hi * di, hr * di - hi * dr)]
        u = dot(jnp.concatenate(parts, 0), fi[...])
        for i in range(2):
            v = [untwist(u[j * R:(j + 1) * R]) for j in (2 * i, 2 * i + 1)]
            y = dot(e2t[...], jnp.concatenate(v, 0)) * SCALE
            osnd[2 * n + i] = y.astype(BF16).reshape(CTX, 8, R)
        if n == 0:
            pltpu.make_async_copy(osnd.at[0, me], out_ref.at[mine], r_out.at[0]).start()
        def send(c, kind):
            i = kind - 2 * n
            remote(osnd.at[kind, c], out_ref.at[mine], s_out.at[0], r_out.at[0], c, sources(n)[i]).start()

        halves((2 * n, 2 * n + 1), send)

    def filter_gradient():
        u = dot(pack(acc[0], acc[1]), fi[...])
        total = dot(e1t[...], untwist(u)) * SCALE
        csnd[...] = total.astype(BF16).reshape(CTX, Q, R)
        place = fil_ref.at[core, me * 4 + zlo]
        pltpu.make_async_copy(csnd.at[me], place, r_c.at[0]).start()
        halves(range(4), lambda c, i: remote(csnd.at[c], place, s_c.at[0], r_c.at[0], c, chips[i]).start())

    analyse(0)
    drain(frcv, r_f.at[0])
    h = dot(twist(dot(e1[...], frcv[...].reshape(CTX * Q, R))), fw[...])
    acc[2], acc[3] = h[:, :R], h[:, R:]
    results(0)
    analyse(1)
    results(1)
    analyse(2)
    results(2)
    analyse(3)
    filter_gradient()
    results(3)

    drain(fil_ref.at[core], r_c.at[0])
    swap = remote(fil_ref.at[core], fil_ref.at[core], s_x.at[0], r_x.at[0], me, mate)
    swap.start()
    drain(out_ref, r_out.at[0])
    swap.wait()

    drain(snd.at[pl.ds(0, CTX * TP - 1)], s_in.at[0])
    drain(snd.at[pl.ds(0, CTX * TP - 1)], s_out.at[0])
    drain(fsnd.at[pl.ds(0, CTX - 1)], s_f.at[0])
    drain(fil_ref.at[0, pl.ds(0, CTX * 4 - 1)], s_c.at[0])


def finish_kernel(o_ref, d_ref, c_ref, k_ref, v_ref, gq_ref, gk_ref, gv_ref, gf_ref, wide, fflat, fwide):
    wide[...] = o_ref[...].astype(F32).reshape(FILTERS * 8, R)
    for q in range(Q):
        lanes = slice(q * R, (q + 1) * R)
        conv = wide[pl.ds(q, FILTERS, stride=8), :]
        grad = wide[pl.ds(Q + q, FILTERS, stride=8), :]
        gq_ref[:, lanes] = (c_ref[:, lanes].astype(F32) * conv).astype(BF16)
        gk_ref[:, lanes] = (v_ref[:, lanes].astype(F32) * grad).astype(BF16)
        gv_ref[:, lanes] = (k_ref[:, lanes].astype(F32) * grad).astype(BF16)
    fflat[...] = d_ref[...].astype(F32).reshape(2, CTX * 4 * Q, R)
    for q in range(Q):
        for k in range(2):
            fwide[pl.ds(k, CTX * 4, stride=2), :] = fflat[k, pl.ds(q, CTX * 4, stride=Q), :]
        gf_ref[:, q * R:(q + 1) * R] = fwide[...].astype(BF16)


def per_device(queries, key_branch, value_branch, filters, cotangent):
    vmem = pl.BlockSpec(memory_space=pltpu.VMEM)
    tabs = [jnp.asarray(t) for t in tables()]
    dma = pltpu.SemaphoreType.DMA
    block = jax.ShapeDtypeStruct((256, TOK), BF16)
    out, fil, key, value, cot = pl.pallas_call(
        exchange_kernel,
        out_shape=(
            jax.ShapeDtypeStruct((FILTERS, 8, R), BF16),
            jax.ShapeDtypeStruct((2, CTX * 4, Q, R), BF16),
            block, block, block,
        ),
        in_specs=[pl.BlockSpec(memory_space=pltpu.HBM)] * 12,
        out_specs=(vmem,) * 5,
        scratch_shapes=[pltpu.VMEM((256, TOK), BF16)] * 2
        + [pltpu.VMEM(t.shape, t.dtype) for t in tabs]
        + [
            dma((12,)),
            pltpu.VMEM((FILTERS, 8, R), BF16),
            pltpu.VMEM((TP, CTX, 8, R), BF16),
            pltpu.VMEM((TP, CTX, 8, R), BF16),
            pltpu.VMEM((CTX, Q, R), BF16),
            pltpu.VMEM((CTX, Q, R), BF16),
            pltpu.VMEM((CTX, Q, R), BF16),
            pltpu.VMEM((FILTERS * 8, R), F32),
            pltpu.VMEM((Q, FILTERS, R), F32),
            pltpu.VMEM((CTX * Q, R), F32),
            pltpu.VMEM((4, R, R), F32),
            pltpu.VMEM((TP, 4, R, R), F32),
            dma((1,)), dma((4, 2)), dma((1,)), dma((1,)), dma((1,)), dma((1,)),
            dma((1,)), dma((1,)), dma((1,)), dma((1,)), pltpu.SemaphoreType.REGULAR,
        ],
        compiler_params=pltpu.CompilerParams(
            collective_id=0, has_side_effects=True, vmem_limit_bytes=40 * 2**20),
        name="exchange",
    )(*(pltpu.with_memory_space_constraint(a, pltpu.HBM)
        for a in (queries, key_branch, value_branch, filters, cotangent, *tabs)))
    return pl.pallas_call(
        finish_kernel,
        out_shape=(block,) * 4,
        in_specs=[vmem] * 5,
        out_specs=(vmem,) * 4,
        scratch_shapes=[
            pltpu.VMEM((FILTERS * 8, R), F32),
            pltpu.VMEM((2, CTX * 4 * Q, R), F32),
            pltpu.VMEM((FILTERS, R), F32),
        ],
        compiler_params=pltpu.CompilerParams(vmem_limit_bytes=32 * 2**20),
        name="finish",
    )(out, fil, cot, key, value)


def solution(mesh):
    placed = (P("tp", "ctx"), P("tp", "ctx"), P("tp", "ctx"), P(None, "ctx"), P("tp", "ctx"))
    return jax.shard_map(
        per_device,
        mesh=mesh,
        in_specs=placed,
        out_specs=(P("tp", "ctx"), P("tp", "ctx"), P("tp", "ctx"), P(None, "ctx")),
        check_vma=False,
    )
```
